128 devices in a mesh: front: 8 (over y, core), row: 4 (over x), col: 4 (over z).
Axes of the slice: x: 4, y: 4, z: 4, core: 2. Of those that a mesh axis runs over, the one named last changes fastest.
Arguments:
- parent_front: float32 [8, 2, 3072, 3072], P('front', None, 'row', 'col'), may hold values from -6 to 6
- child_left: bfloat16 [3584, 256, 256], P(('front', 'row', 'col')), may hold values from -0.375 to 0.375
- child_right: bfloat16 [3584, 256, 256], P(('front', 'row', 'col')), may hold values from -6 to 6
- tile_ranks: int32 [3584], P(('front', 'row', 'col')), may hold values from 1 to 128, as said below
- destination: int32 [3584], P(('front', 'row', 'col')), may hold values from 0 to 31, as said below
- tile_place: int32 [3584], P(('front', 'row', 'col')), may hold values from 0 to 8
- row_source: int32 [3584, 256], P(('front', 'row', 'col')), may hold values from 0 to 255, each once within a row
- col_source: int32 [3584, 256], P(('front', 'row', 'col')), may hold values from 0 to 255, each once within a row
- own_left: bfloat16 [512, 256, 256], P(('front', 'row', 'col')), may hold values from -0.375 to 0.375
- own_right: bfloat16 [512, 256, 256], P(('front', 'row', 'col')), may hold values from -6 to 6
- own_place: int32 [512], P(('front', 'row', 'col')), may hold values from 0 to 8
- pivot_inverse: float32 [8, 3, 2, 256, 256], P('front'), may hold values from -0.01171875 to 0.01171875
Outputs:
- factored: float32 [8, 2, 3072, 3072], P('front', None, 'row', 'col')
The draws below stay inside these ranges and needn't reach their ends.
Inputs may be any that keep to these rules, and one draw needn't show every extreme that they name: `tile_ranks`: every device's tiles include one of rank 128. A destination d means front d // (row axis size) and row d mod (row axis size) in the sender's own column. No device sends more than 2 tiles to one destination; in every column one destination receives exactly 2 tiles from every device of that column.
All inputs are finite; a program needn't handle non-finite values.
Results may differ from the reference program's by a relative error of at most 0.0003.
Values may be sent and summed in bfloat16 or wider, within the bound.
No kernel may reach another device: no remote copies, remote signals or barrier semaphores. Data moves between devices by JAX's collectives and lax.ppermute only.
A program may use at most 192 MiB of HBM per device.

```python
import math
import jax
import jax.numpy as jnp
from jax import lax

TILE = 256
RANK = 128
CAP = 2
TS = 3
PANELS = 3
OWN = 4
KT = 28
CHILDREN = 3584
OWNED = 512
FRONTS = 8
FW = 3072
N_FRONT = 8
N_ROW = 4
N_COL = 4
DEVICES = 128


def draw_tile_ranks(key, part):
    key = jax.random.fold_in(key, 11)
    drawn = jax.random.randint(key, (CHILDREN,), 1, RANK + 1)
    leading = jnp.arange(CHILDREN) % KT == 0
    return jnp.where(leading, RANK, drawn).astype(jnp.int32)


def draw_destination(key, part):
    key = jax.random.fold_in(key, 23)
    groups_count = N_FRONT * N_ROW
    hot_dest = jax.random.randint(jax.random.fold_in(key, 1), (N_COL,), 0, groups_count)

    def per_device(device):
        subkey = jax.random.fold_in(key, device + 7)
        hottest = hot_dest[device % N_COL]
        indices = jnp.arange(groups_count - 1)
        others = indices + (indices >= hottest).astype(indices.dtype)
        source_pool = jnp.tile(others, CAP)
        chosen = jax.random.permutation(jax.random.fold_in(subkey, 1), source_pool)[:KT - CAP]
        listing = jnp.concatenate([jnp.full((CAP,), 0, jnp.int32) + hottest.astype(jnp.int32), chosen.astype(jnp.int32)])
        return jax.random.permutation(jax.random.fold_in(subkey, 2), listing)
    return jax.vmap(per_device)(jnp.arange(DEVICES)).reshape(-1).astype(jnp.int32)


def place_ends(values, own_key, smallest, top_value):
    index_at = [jax.random.randint(jax.random.fold_in(own_key, axis), (), 0, length) for axis, length in enumerate(values.shape)]
    widest = values.shape.index(max(values.shape))
    beside = index_at[:widest] + [(index_at[widest] + 1) % values.shape[widest]] + index_at[widest + 1:]
    return values.at[tuple(index_at)].set(smallest).at[tuple(beside)].set(top_value)


def levels(rng, dims, split, low, high):
    loudness = 1.0
    for axis_at, blocks in split:
        draws = jax.random.uniform(jax.random.fold_in(jax.random.fold_in(rng, 6), axis_at), (blocks,), jnp.float32, low / len(split), high / len(split))
        loudness = loudness * jnp.repeat(jnp.exp(draws), dims[axis_at] // blocks).reshape((-1,) + (1,) * (len(dims) - 1 - axis_at))
    return loudness


def centred(key, dims, scale, limit, cuts=(), kind=jnp.bfloat16):
    factor_of = levels(key, dims, cuts, -0.22, 0.18) if cuts else 1.0
    values = jax.random.normal(key, dims, jnp.float32) * scale * factor_of
    return jnp.minimum(jnp.maximum(values, -limit), limit).astype(kind)


def setup_inputs(seed: int = 0) -> dict:
    keys = jax.random.split(jax.random.key(seed), 13)
    parent_front = centred(keys[0], (FRONTS, 2, FW, FW), 1.0, 6.0, ((0, 8), (2, 4), (3, 4)), jnp.float32)
    child_left = centred(keys[1], (CHILDREN, TILE, 2 * RANK), (2 * RANK) ** -0.5, 0.375, ((0, 128),))
    child_right = centred(keys[2], (CHILDREN, TILE, 2 * RANK), 1.0, 6.0, ((0, 128),))
    tile_ranks = draw_tile_ranks(jax.random.fold_in(keys[12], 71), 0)
    destination = draw_destination(jax.random.fold_in(keys[12], 71), 0)
    tile_place = place_ends(jax.random.randint(keys[5], (CHILDREN,), 0, TS * TS), jax.random.fold_in(keys[5], 1), 0, (TS * TS) - 1).astype(jnp.int32)
    row_source = jax.vmap(lambda own: jax.random.permutation(own, TILE))(jax.random.split(keys[6], CHILDREN)).reshape((CHILDREN, TILE)).astype(jnp.int32)
    col_source = jax.vmap(lambda own: jax.random.permutation(own, TILE))(jax.random.split(keys[7], CHILDREN)).reshape((CHILDREN, TILE)).astype(jnp.int32)
    own_left = centred(keys[8], (OWNED, TILE, 2 * RANK), (2 * RANK) ** -0.5, 0.375, ((0, 128),))
    own_right = centred(keys[9], (OWNED, TILE, 2 * RANK), 1.0, 6.0, ((0, 128),))
    own_place = place_ends(jax.random.randint(keys[10], (OWNED,), 0, TS * TS), jax.random.fold_in(keys[10], 1), 0, (TS * TS) - 1).astype(jnp.int32)
    pivot_inverse = centred(keys[11], (FRONTS, PANELS, 2, TILE, TILE), (4 * TILE * TILE) ** -0.5, 0.01171875, ((0, 8),), jnp.float32)
    return dict(parent_front=parent_front, child_left=child_left, child_right=child_right, tile_ranks=tile_ranks, destination=destination, tile_place=tile_place, row_source=row_source, col_source=col_source, own_left=own_left, own_right=own_right, own_place=own_place, pivot_inverse=pivot_inverse)


def complex_mult(left, right):
    highest = lax.Precision.HIGHEST
    real_part = jnp.dot(left[0], right[0], precision=highest) - jnp.dot(left[1], right[1], precision=highest)
    imag_part = jnp.dot(left[0], right[1], precision=highest) + jnp.dot(left[1], right[0], precision=highest)
    return jnp.stack([real_part, imag_part])


def pick_rows(block, chosen):
    return block[chosen]


def scatter_updates(front_tiles, lefts, rights, targets):
    item_count = lefts.shape[0]
    block_size = math.gcd(item_count, 64)
    blocks = item_count // block_size

    def add_block(running, pieces):
        left_block, right_block, target_block = pieces
        real_side = jnp.concatenate([right_block[..., :RANK], -right_block[..., RANK:]], -1)
        imag_side = jnp.concatenate([right_block[..., RANK:], right_block[..., :RANK]], -1)
        both_sides = jnp.stack([real_side, imag_side], 1)
        update = jnp.einsum("skq,sclq->sckl", left_block.astype(jnp.float32), both_sides.astype(jnp.float32), precision=lax.Precision.HIGHEST)
        return running.at[target_block].add(update), None

    pieces = (lefts.reshape((blocks, block_size) + lefts.shape[1:]),
              rights.reshape((blocks, block_size) + rights.shape[1:]),
              targets.reshape(blocks, block_size))
    result, unused = lax.scan(add_block, front_tiles, pieces)
    return result


def factor_front(pieces):
    matrix, inverses = pieces
    for panel in range(PANELS):
        first_col = panel * TILE
        end_col = first_col + TILE
        factor = complex_mult(matrix[:, :, first_col:end_col], inverses[panel])
        product = complex_mult(factor[:, end_col:, :], matrix[:, first_col:end_col, end_col:])
        matrix = matrix.at[:, end_col:, end_col:].set(matrix[:, end_col:, end_col:] - product)
        matrix = matrix.at[:, end_col:, first_col:end_col].set(factor[:, end_col:, :])
    return matrix


def reference(parent_front, child_left, child_right, tile_ranks, destination, tile_place, row_source, col_source, own_left, own_right, own_place, pivot_inverse):
    across = TS * N_ROW
    fronts_count = parent_front.shape[0]
    order_full = parent_front.shape[2]
    front_tiles = parent_front.reshape(fronts_count, 2, across, TILE, across, TILE).transpose(0, 2, 4, 1, 3, 5)
    front_tiles = front_tiles.reshape(fronts_count * across * across, 2, TILE, TILE)

    width_index = (jnp.arange(2 * RANK) % RANK).astype(jnp.int32)
    keep = width_index[None, None, :] < tile_ranks[:, None, None]
    masked = jnp.where(keep, child_left, jnp.zeros((), child_left.dtype))
    left_ready = jax.vmap(pick_rows)(masked, row_source)
    right_ready = jax.vmap(pick_rows)(child_right, col_source)
    positions = jnp.arange(CHILDREN).astype(jnp.int32)
    holder_col = (positions // KT) % N_COL
    tile_row = (destination % N_ROW) * TS + tile_place // TS
    tile_col = holder_col * TS + tile_place % TS
    targets = (((destination // N_ROW) * across + tile_row) * across + tile_col).astype(jnp.int32)
    front_tiles = scatter_updates(front_tiles, left_ready, right_ready, targets)

    owners = jnp.arange(OWNED).astype(jnp.int32) // OWN
    owner_front = owners // (N_ROW * N_COL)
    owner_row = (owners // N_COL) % N_ROW
    owner_col = owners % N_COL
    own_targets = ((owner_front * across + owner_row * TS + own_place // TS) * across + owner_col * TS + own_place % TS).astype(jnp.int32)
    front_tiles = scatter_updates(front_tiles, own_left, own_right, own_targets)

    assembled = front_tiles.reshape(fronts_count, across, across, 2, TILE, TILE).transpose(0, 3, 1, 4, 2, 5)
    assembled = assembled.reshape(fronts_count, 2, order_full, order_full)
    return lax.map(factor_front, (assembled, pivot_inverse))
```

```python
import functools
import math

import jax
import jax.numpy as jnp
from jax import lax
from jax.experimental import pallas as pl
from jax.experimental.pallas import tpu as pltpu
from jax.sharding import PartitionSpec as P

TILE = 256
RANK = 128
TS = 3
SIDE = TS * TILE
SENT = 28
GROUP = 32
RING = 4
CODE_ROWS = 16
LOG_STEP = math.log(2.0) / 32.0
VMEM_BYTES = 48 * 1024 * 1024
BF16 = jnp.bfloat16
F32 = jnp.float32


def encode(values):
    peak = jnp.maximum(jnp.max(jnp.abs(values), axis=0, keepdims=True), 1e-30)
    code = jnp.ceil(jnp.log(peak * (1.0 / 32700.0)) * (1.0 / LOG_STEP))
    whole = jnp.round(values * jnp.exp(code * -LOG_STEP))
    whole = jnp.clip(whole, -32767.0, 32767.0).astype(jnp.int32)
    code_rows = jnp.broadcast_to(code.astype(jnp.int32), (CODE_ROWS, values.shape[1]))
    return whole.astype(jnp.int16), code_rows.astype(jnp.int16)


def store_piece(ref, piece, values):
    rows = values.shape[0]
    whole, code_rows = encode(values)
    ref[piece, :rows, :] = whole
    ref[piece, rows:, :] = code_rows


def decode(piece_rows, code_rows):
    code = code_rows[:1].astype(jnp.int32).astype(F32)
    return piece_rows.astype(jnp.int32).astype(F32) * jnp.exp(code * LOG_STEP)


def cut(x):
    high = x.astype(BF16)
    return high, (x - high.astype(F32)).astype(BF16)


def dot(a, b):
    return lax.dot_general(a, b, (((1,), (0,)), ((), ())), preferred_element_type=F32)


def dot_cut(a, b):
    return dot(a[0], b[0]) + (dot(a[0], b[1]) + dot(a[1], b[0]))


def complex_dot(a, b):
    a = [cut(x) for x in a]
    b = [cut(x) for x in b]
    return (
        dot_cut(a[0], b[0]) - dot_cut(a[1], b[1]),
        dot_cut(a[0], b[1]) + dot_cut(a[1], b[0]),
    )


def minus(a, b):
    return a[0] - b[0], a[1] - b[1]


def pack_kernel(source, filled, ranks, left, right, rows, cols, out):
    slot = pl.program_id(0)

    @pl.when(filled[slot] == 1)
    def _():
        rank = ranks[source[slot]]
        index = lax.broadcasted_iota(jnp.int32, (TILE, TILE), 0)

        def picked(chosen, block):
            onehot = jnp.where(index == chosen, 1.0, 0.0).astype(BF16)
            return lax.dot_general(
                onehot, block, (((0,), (0,)), ((), ())), preferred_element_type=F32
            )

        width = lax.broadcasted_iota(jnp.int32, (TILE, 2 * RANK), 1)
        width = jnp.where(width >= RANK, width - RANK, width)
        moved = picked(rows[0], left[0])
        out[0, :TILE, :] = jnp.where(width < rank, moved, 0.0).astype(BF16)
        out[0, TILE:, :] = picked(cols[0], right[0]).astype(BF16)


def pack(source, filled, ranks, left, right, rows, cols):
    tile = pl.BlockSpec((1, TILE, 2 * RANK), lambda s, src, fil, rnk: (src[s], 0, 0))
    line = pl.BlockSpec((1, 1, TILE), lambda s, src, fil, rnk: (src[s], 0, 0))
    return pl.pallas_call(
        pack_kernel,
        grid_spec=pltpu.PrefetchScalarGridSpec(
            num_scalar_prefetch=3,
            grid=(GROUP,),
            in_specs=[tile, tile, line, line],
            out_specs=pl.BlockSpec(
                (1, 2 * TILE, 2 * RANK), lambda s, src, fil, rnk: (s, 0, 0)
            ),
        ),
        out_shape=jax.ShapeDtypeStruct((GROUP, 2 * TILE, 2 * RANK), BF16),
        compiler_params=pltpu.CompilerParams(vmem_limit_bytes=VMEM_BYTES),
        cost_estimate=pl.CostEstimate(
            flops=4 * SENT * TILE**3, bytes_accessed=16 * 2**20, transcendentals=0
        ),
    )(source, filled, ranks, left, right, rows, cols)


def add_tile(out, place, left, right):
    real_side = jnp.concatenate([right[:, :RANK], -right[:, RANK:]], 1)
    imag_side = jnp.concatenate([right[:, RANK:], right[:, :RANK]], 1)
    a = place // TS
    rows = pl.ds(pl.multiple_of(a * TILE, TILE), TILE)
    cols = pl.ds(pl.multiple_of((place - a * TS) * TILE, TILE), TILE)
    contract = (((1,), (1,)), ((), ()))
    out[0, rows, cols] += lax.dot_general(left, real_side, contract, preferred_element_type=F32)
    out[1, rows, cols] += lax.dot_general(left, imag_side, contract, preferred_element_type=F32)


def first_kernel(block_of, places, own_places, before, own_left, own_right, slots, out):
    step = pl.program_id(0)

    @pl.when(step == 0)
    def _():
        out[...] = before[...]

        def own_step(j, carry):
            add_tile(out, own_places[j], own_left[j], own_right[j])
            return carry

        lax.fori_loop(0, own_left.shape[0], own_step, 0)

    @pl.when(places[step] >= 0)
    def _():
        add_tile(out, places[step], slots[0, :TILE, :], slots[0, TILE:, :])


def second_kernel(block_of, places, role, before, slots, inverse, out, upper, lower):
    step = pl.program_id(0)

    @pl.when(step == 0)
    def _():
        out[...] = before[...]

    @pl.when(places[step] >= 0)
    def _():
        add_tile(out, places[step], slots[0, :TILE, :], slots[0, TILE:, :])

    @pl.when((step == GROUP - 1) & (role[0] == 0) & (role[1] == 0))
    def _():
        def at(i, j):
            rows, cols = slice(i * TILE, (i + 1) * TILE), slice(j * TILE, (j + 1) * TILE)
            return out[0, rows, cols], out[1, rows, cols]

        def put(i, j, value):
            rows, cols = slice(i * TILE, (i + 1) * TILE), slice(j * TILE, (j + 1) * TILE)
            out[0, rows, cols] = value[0]
            out[1, rows, cols] = value[1]

        for p in range(TS - 1):
            pivot = inverse[p, 0], inverse[p, 1]
            for i in range(p + 1, TS):
                factor = complex_dot(at(i, p), pivot)
                put(i, p, factor)
                for j in range(p + 1, TS):
                    put(i, j, minus(at(i, j), complex_dot(factor, at(p, j))))

        quarter = TILE // RING
        for piece in range(RING):
            part = slice(piece * quarter, (piece + 1) * quarter)
            for ref, tiles in ((upper, ((0, 1), (0, 2), (1, 2))), (lower, ((1, 0), (2, 0), (2, 1)))):
                wide = jnp.concatenate([x[part] for ij in tiles for x in at(*ij)], 1)
                store_piece(ref, piece, wide)


def whole(shape):
    return pl.BlockSpec(shape, lambda *_: (0,) * len(shape))


def slot_spec():
    return pl.BlockSpec((1, 2 * TILE, 2 * RANK), lambda s, blk, *_: (blk[s], 0, 0))


ADD_COST = pl.CostEstimate(
    flops=4 * GROUP * TILE**3, bytes_accessed=20 * 2**20, transcendentals=0
)


def add_first(block_of, places, own_places, before, own_left, own_right, slots):
    return pl.pallas_call(
        first_kernel,
        grid_spec=pltpu.PrefetchScalarGridSpec(
            num_scalar_prefetch=3,
            grid=(GROUP,),
            in_specs=[
                whole(before.shape),
                whole(own_left.shape),
                whole(own_right.shape),
                slot_spec(),
            ],
            out_specs=whole(before.shape),
        ),
        out_shape=jax.ShapeDtypeStruct(before.shape, F32),
        compiler_params=pltpu.CompilerParams(vmem_limit_bytes=VMEM_BYTES),
        cost_estimate=ADD_COST,
    )(block_of, places, own_places, before, own_left, own_right, slots)


def small_shape():
    return (RING, TILE // RING + CODE_ROWS, 2 * TS * TILE)


def add_second(block_of, places, role, before, slots, inverse):
    return pl.pallas_call(
        second_kernel,
        grid_spec=pltpu.PrefetchScalarGridSpec(
            num_scalar_prefetch=3,
            grid=(GROUP,),
            in_specs=[whole(before.shape), slot_spec(), whole(inverse.shape)],
            out_specs=[whole(before.shape), whole(small_shape()), whole(small_shape())],
        ),
        out_shape=[
            jax.ShapeDtypeStruct(before.shape, F32),
            jax.ShapeDtypeStruct(small_shape(), jnp.int16),
            jax.ShapeDtypeStruct(small_shape(), jnp.int16),
        ],
        compiler_params=pltpu.CompilerParams(vmem_limit_bytes=VMEM_BYTES),
        cost_estimate=ADD_COST,
    )(block_of, places, role, before, slots, inverse)


def gather_pieces(refs, place, rows, put):
    own, below, above, far_top, far_bottom = refs
    half = far_top.shape[0]

    def at(shift):
        return (place + shift) & (RING - 1)

    put(at(0) * rows, decode(own[:rows, :], own[rows:, :]))
    put(at(RING - 1) * rows, decode(below[:rows, :], below[rows:, :]))
    put(at(1) * rows, decode(above[:rows, :], above[rows:, :]))
    codes = far_bottom[rows - half :, :]
    put(at(2) * rows, decode(far_top[...], codes))
    put(at(2) * rows + half, decode(far_bottom[: rows - half, :], codes))


def panel_kernel(role, block, inverse, *refs):
    uppers, lowers = refs[:5], refs[5:10]
    out, left_coded, right_coded, held, wide = refs[10:]
    quarter = TILE // RING

    def fill(pieces, place):
        def put(start, values):
            wide[pl.ds(pl.multiple_of(start, 8), values.shape[0]), :] = values

        gather_pieces(pieces, place, quarter, put)

    def small(t):
        first = 2 * t * TILE
        return wide[:, first : first + TILE], wide[:, first + TILE : first + 2 * TILE]

    def pivot(p):
        return inverse[p, 0], inverse[p, 1]

    @pl.when((role[0] > 0) & (role[1] == 0))
    def _():
        pltpu.sync_copy(block, held)
        fill(uppers, role[0])

        def chunk(i, carry):
            rows = pl.ds(pl.multiple_of(i * TILE, TILE), TILE)

            def at(j):
                cols = slice(j * TILE, (j + 1) * TILE)
                return held[0, rows, cols], held[1, rows, cols]

            f0 = complex_dot(at(0), pivot(0))
            f1 = complex_dot(minus(at(1), complex_dot(f0, small(0))), pivot(1))
            a2 = minus(at(2), complex_dot(f0, small(1)))
            a2 = minus(a2, complex_dot(f1, small(2)))
            for j, f in enumerate((f0, f1, complex_dot(a2, pivot(2)))):
                cols = slice(j * TILE, (j + 1) * TILE)
                held[0, rows, cols] = f[0]
                held[1, rows, cols] = f[1]
            return carry

        lax.fori_loop(0, TS, chunk, 0)
        pltpu.sync_copy(held, out)
        part = SIDE // RING

        def code_piece(piece, carry):
            rows = pl.ds(pl.multiple_of(piece * part, 8), part)
            store_piece(
                left_coded, piece, jnp.concatenate([held[0, rows, :], held[1, rows, :]], 1)
            )
            return carry

        lax.fori_loop(0, RING, code_piece, 0)

    @pl.when((role[0] == 0) & (role[1] > 0))
    def _():
        pltpu.sync_copy(block, held)
        fill(lowers, role[1])

        def chunk(j, carry):
            cols = pl.ds(pl.multiple_of(j * TILE, TILE), TILE)

            def at(i):
                rows = slice(i * TILE, (i + 1) * TILE)
                return held[0, rows, cols], held[1, rows, cols]

            p0 = at(0)
            p1 = minus(at(1), complex_dot(small(0), p0))
            p2 = minus(at(2), complex_dot(small(1), p0))
            p2 = minus(p2, complex_dot(small(2), p1))
            for i, p in ((1, p1), (2, p2)):
                rows = slice(i * TILE, (i + 1) * TILE)
                held[0, rows, cols] = p[0]
                held[1, rows, cols] = p[1]
            return carry

        lax.fori_loop(0, TS, chunk, 0)
        pltpu.sync_copy(held, out)
        part = 2 * SIDE // RING
        for piece in range(RING):
            half, start = divmod(piece * part, SIDE)
            store_piece(right_coded, piece, held[half, start : start + part, :])


def left_shape():
    return (RING, SIDE // RING + CODE_ROWS, 2 * SIDE)


def right_shape():
    return (RING, 2 * SIDE // RING + CODE_ROWS, SIDE)


def panel(role, block, inverse, uppers, lowers):
    anywhere = pl.BlockSpec(memory_space=pl.ANY)
    held = pl.BlockSpec(memory_space=pltpu.VMEM)
    return pl.pallas_call(
        panel_kernel,
        in_specs=[pl.BlockSpec(memory_space=pltpu.SMEM), anywhere] + [held] * 11,
        out_specs=[anywhere, held, held],
        out_shape=[
            jax.ShapeDtypeStruct(block.shape, F32),
            jax.ShapeDtypeStruct(left_shape(), jnp.int16),
            jax.ShapeDtypeStruct(right_shape(), jnp.int16),
        ],
        scratch_shapes=[
            pltpu.VMEM(block.shape, F32),
            pltpu.VMEM((TILE, 2 * TS * TILE), F32),
        ],
        input_output_aliases={1: 0},
        compiler_params=pltpu.CompilerParams(vmem_limit_bytes=VMEM_BYTES),
    )(role, block, inverse, *uppers, *lowers)


def trail_kernel(role, block, *refs):
    lefts, rights = refs[:5], refs[5:10]
    out, held, left_high, left_low, right_high, right_low, sem = refs[10:]

    @pl.when((role[0] > 0) & (role[1] > 0))
    def _():
        fetch = pltpu.make_async_copy(block, held, sem)
        fetch.start()

        def into(high, low):
            def put(start, values):
                rows = pl.ds(pl.multiple_of(start, 16), values.shape[0])
                h, l = cut(values)
                high[rows, :] = h
                low[rows, :] = l

            return put

        gather_pieces(lefts, role[1], SIDE // RING, into(left_high, left_low))
        gather_pieces(rights, role[0], 2 * SIDE // RING, into(right_high, right_low))
        fetch.wait()

        def chunk(i, carry):
            rows = pl.ds(pl.multiple_of(i * TILE, TILE), TILE)
            high, low = left_high[rows, :], left_low[rows, :]

            def real_of(x):
                return jnp.concatenate([x[:, :SIDE], -x[:, SIDE:]], 1)

            def imag_of(x):
                return jnp.concatenate([x[:, SIDE:], x[:, :SIDE]], 1)

            for half, form in ((0, real_of), (1, imag_of)):
                h, l = form(high), form(low)
                for j in range(TS):
                    cols = slice(j * TILE, (j + 1) * TILE)
                    b = right_high[:, cols], right_low[:, cols]
                    held[half, rows, cols] -= dot_cut((h, l), b)
            return carry

        lax.fori_loop(0, TS, chunk, 0)
        pltpu.sync_copy(held, out)


def trail(role, block, lefts, rights):
    anywhere = pl.BlockSpec(memory_space=pl.ANY)
    held = pl.BlockSpec(memory_space=pltpu.VMEM)
    return pl.pallas_call(
        trail_kernel,
        in_specs=[pl.BlockSpec(memory_space=pltpu.SMEM), anywhere] + [held] * 10,
        out_specs=anywhere,
        out_shape=jax.ShapeDtypeStruct(block.shape, F32),
        scratch_shapes=[
            pltpu.VMEM(block.shape, F32),
            pltpu.VMEM((SIDE, 2 * SIDE), BF16),
            pltpu.VMEM((SIDE, 2 * SIDE), BF16),
            pltpu.VMEM((2 * SIDE, SIDE), BF16),
            pltpu.VMEM((2 * SIDE, SIDE), BF16),
            pltpu.SemaphoreType.DMA,
        ],
        input_output_aliases={1: 0},
        compiler_params=pltpu.CompilerParams(vmem_limit_bytes=VMEM_BYTES),
    )(role, block, *lefts, *rights)


def spread(pieces, axis):
    got = [lax.ppermute(pieces[d], axis, [(0, d)]) for d in (1, 3, 2)]
    here = lax.axis_index(axis)
    return jnp.where(
        here == 0,
        pieces[0],
        jnp.where(here == 1, got[0], jnp.where(here == 3, got[1], got[2])),
    )


def ring(own, axis, rows):
    up = [(i, (i + 1) % RING) for i in range(RING)]
    down = [(i, (i - 1) % RING) for i in range(RING)]
    half = rows // 2 // 16 * 16
    below = lax.ppermute(own, axis, up)
    above = lax.ppermute(own, axis, down)
    far_top = lax.ppermute(below[:half], axis, up)
    far_bottom = lax.ppermute(above[half:], axis, down)
    return own, below, above, far_top, far_bottom


def body(
    parent_front,
    child_left,
    child_right,
    tile_ranks,
    destination,
    tile_place,
    row_source,
    col_source,
    own_left,
    own_right,
    own_place,
    pivot_inverse,
):
    joined = ("front", "row")
    me = lax.axis_index(joined)
    role = jnp.stack([lax.axis_index("row"), lax.axis_index("col")]).astype(jnp.int32)
    none = 16 * SENT
    numbered = 16 * jnp.arange(SENT, dtype=jnp.int32) + tile_place

    told = lax.all_gather(destination * 16 + tile_place, joined)
    told_place = told & 15
    told_number = 16 * jnp.arange(SENT, dtype=jnp.int32)[None, :] + told_place
    to_me = jnp.where((told >> 4) == me, told_number, none)
    first_in = jnp.min(to_me, 1)
    second_in = jnp.min(jnp.where(to_me > first_in[:, None], to_me, none), 1)

    to_each = jnp.where(
        destination[None, :] == jnp.arange(GROUP, dtype=jnp.int32)[:, None],
        numbered[None, :],
        none,
    )
    first_out = jnp.min(to_each, 1)
    second_out = jnp.min(jnp.where(to_each > first_out[:, None], to_each, none), 1)

    rows = row_source[:, None, :]
    cols = col_source[:, None, :]
    slots = []
    for number in (first_out, second_out):
        filled = (number < none).astype(jnp.int32)
        slots.append(
            pack((number >> 4) * filled, filled, tile_ranks, child_left, child_right, rows, cols)
        )
    first_slots = lax.all_to_all(slots[0], joined, split_axis=0, concat_axis=0, tiled=True)
    second_slots = lax.all_to_all(slots[1], joined, split_axis=0, concat_axis=0, tiled=True)

    def places_of(number):
        filled = number < none
        block_of = jnp.where(filled, jnp.arange(GROUP, dtype=jnp.int32), 0)
        return block_of, jnp.where(filled, number & 15, -1)

    inverse = pivot_inverse[0]
    block = add_first(
        *places_of(first_in), own_place, parent_front[0], own_left, own_right, first_slots
    )
    block, upper, lower = add_second(
        *places_of(second_in), role, block, second_slots, inverse
    )
    uppers = ring(spread(upper, "row"), "row", TILE // RING)
    lowers = ring(spread(lower, "col"), "col", TILE // RING)
    block, left, right = panel(role, block, inverse, uppers, lowers)
    lefts = ring(spread(left, "col"), "col", SIDE // RING)
    rights = ring(spread(right, "row"), "row", 2 * SIDE // RING)
    return trail(role, block, lefts, rights)[None]


def solution(mesh):
    joined = ("front", "row", "col")
    tiles = P(joined, None, None)
    return jax.shard_map(
        body,
        mesh=mesh,
        in_specs=(
            P("front", None, "row", "col"),
            tiles,
            tiles,
            P(joined),
            P(joined),
            P(joined),
            P(joined, None),
            P(joined, None),
            tiles,
            tiles,
            P(joined),
            P("front", None, None, None, None),
        ),
        out_specs=P("front", None, "row", "col"),
        check_vma=False,
    )
```

```python
import functools
import math

import jax
import jax.numpy as jnp
from jax import lax
from jax.experimental import pallas as pl
from jax.experimental.pallas import tpu as pltpu
from jax.sharding import PartitionSpec as P

TILE = 256
RANK = 128
TS = 3
SIDE = TS * TILE
SENT = 28
GROUP = 32
RING = 4
CODE_ROWS = 16
STEP = 4
NOTE_ROWS = 16
LOG_STEP = math.log(2.0) / 32.0
VMEM_BYTES = 48 * 1024 * 1024
BF16 = jnp.bfloat16
F32 = jnp.float32


def encode(values):
    peak = jnp.maximum(jnp.max(jnp.abs(values), axis=0, keepdims=True), 1e-30)
    code = jnp.ceil(jnp.log(peak * (1.0 / 32700.0)) * (1.0 / LOG_STEP))
    whole = jnp.round(values * jnp.exp(code * -LOG_STEP))
    whole = jnp.clip(whole, -32767.0, 32767.0).astype(jnp.int32)
    code_rows = jnp.broadcast_to(code.astype(jnp.int32), (CODE_ROWS, values.shape[1]))
    return whole.astype(jnp.int16), code_rows.astype(jnp.int16)


def store_piece(ref, piece, values):
    rows = values.shape[0]
    whole, code_rows = encode(values)
    ref[piece, :rows, :] = whole
    ref[piece, rows:, :] = code_rows


def decode(piece_rows, code_rows):
    code = code_rows[:1].astype(jnp.int32).astype(F32)
    return piece_rows.astype(jnp.int32).astype(F32) * jnp.exp(code * LOG_STEP)


def cut(x):
    high = x.astype(BF16)
    return high, (x - high.astype(F32)).astype(BF16)


def dot(a, b):
    return lax.dot_general(a, b, (((1,), (0,)), ((), ())), preferred_element_type=F32)


def dot_cut(a, b):
    return dot(a[0], b[0]) + (dot(a[0], b[1]) + dot(a[1], b[0]))


def cuts(pair):
    return [cut(x) for x in pair]


def complex_dot(a, b):
    return (
        dot_cut(a[0], b[0]) - dot_cut(a[1], b[1]),
        dot_cut(a[0], b[1]) + dot_cut(a[1], b[0]),
    )


def minus(a, b):
    return a[0] - b[0], a[1] - b[1]


def pack_kernel(told, source, filled, ranks, *notes_and_refs):
    notes, refs = notes_and_refs[:told], notes_and_refs[told:]
    lefts, rights, rows, cols = (refs[STEP * i : STEP * (i + 1)] for i in range(4))
    out = refs[4 * STEP]
    first = pl.program_id(0) * STEP
    index = lax.broadcasted_iota(jnp.int32, (TILE, TILE), 0)
    width = lax.broadcasted_iota(jnp.int32, (TILE, 2 * RANK), 1)
    width = jnp.where(width >= RANK, width - RANK, width)
    turned = (((0,), (0,)), ((), ()))

    def onehot(chosen):
        return jnp.where(index == chosen, 1.0, 0.0).astype(BF16)

    for j in range(STEP):
        if told:
            at = lax.broadcasted_iota(jnp.int32, (NOTE_ROWS, TILE), 0)
            lines = jnp.where(at == 0, notes[0][first + j], notes[1][first + j])
            out[j, TILE + 2 * RANK :, :] = lines.astype(F32).astype(BF16)

        @pl.when(filled[first + j] == 1)
        def _(j=j):
            rank = ranks[source[first + j]]
            moved = lax.dot_general(
                onehot(rows[j][0]), lefts[j][0], turned, preferred_element_type=F32
            )
            out[j, :TILE, :] = jnp.where(width < rank, moved, 0.0).astype(BF16)
            out[j, TILE : TILE + 2 * RANK, :] = lax.dot_general(
                rights[j][0], onehot(cols[j][0]), turned, preferred_element_type=F32
            ).astype(BF16)


def pack(source, filled, ranks, notes, left, right, rows, cols):
    depth = TILE + 2 * RANK + (NOTE_ROWS if notes else 0)

    def spec(shape, j):
        return pl.BlockSpec((1,) + shape, lambda s, src, *_: (src[s * STEP + j], 0, 0))

    tiles = [spec((TILE, 2 * RANK), j) for j in range(STEP)]
    lines = [spec((1, TILE), j) for j in range(STEP)]
    return pl.pallas_call(
        functools.partial(pack_kernel, len(notes)),
        grid_spec=pltpu.PrefetchScalarGridSpec(
            num_scalar_prefetch=3 + len(notes),
            grid=(GROUP // STEP,),
            in_specs=tiles + tiles + lines + lines,
            out_specs=pl.BlockSpec((STEP, depth, TILE), lambda s, *_: (s, 0, 0)),
        ),
        out_shape=jax.ShapeDtypeStruct((GROUP, depth, TILE), BF16),
        compiler_params=pltpu.CompilerParams(vmem_limit_bytes=VMEM_BYTES),
        cost_estimate=pl.CostEstimate(
            flops=4 * SENT * TILE**3, bytes_accessed=16 * 2**20, transcendentals=0
        ),
    )(source, filled, ranks, *notes, *[left] * STEP, *[right] * STEP, *[rows] * STEP, *[cols] * STEP)


def add_at(out, place, real, imag):
    a = place // TS
    rows = pl.ds(pl.multiple_of(a * TILE, TILE), TILE)
    cols = pl.ds(pl.multiple_of((place - a * TS) * TILE, TILE), TILE)
    out[0, rows, cols] += real
    out[1, rows, cols] += imag


def add_own(out, place, left, right):
    real_side = jnp.concatenate([right[:, :RANK], -right[:, RANK:]], 1)
    imag_side = jnp.concatenate([right[:, RANK:], right[:, :RANK]], 1)
    contract = (((1,), (1,)), ((), ()))
    add_at(
        out,
        place,
        lax.dot_general(left, real_side, contract, preferred_element_type=F32),
        lax.dot_general(left, imag_side, contract, preferred_element_type=F32),
    )


def add_slots(out, places, slots):
    first = pl.program_id(0) * STEP
    for j in range(STEP):

        @pl.when(places[first + j] >= 0)
        def _(j=j):
            left = slots[j, :TILE, :]
            top = slots[j, TILE : TILE + RANK, :]
            bottom = slots[j, TILE + RANK : TILE + 2 * RANK, :]
            add_at(
                out,
                places[first + j],
                dot(left, jnp.concatenate([top, -bottom], 0)),
                dot(left, jnp.concatenate([bottom, top], 0)),
            )


def first_kernel(places, own_places, before, own_left, own_right, slots, out):
    @pl.when(pl.program_id(0) == 0)
    def _():
        pltpu.sync_copy(before, out)

        def own_step(j, carry):
            add_own(out, own_places[j], own_left[j], own_right[j])
            return carry

        lax.fori_loop(0, own_left.shape[0], own_step, 0)

    add_slots(out, places, slots)


def tile_at(i, j):
    return slice(i * TILE, (i + 1) * TILE), slice(j * TILE, (j + 1) * TILE)


def get(ref, rows, cols):
    return ref[0, rows, cols], ref[1, rows, cols]


def put(ref, rows, cols, value):
    ref[0, rows, cols] = value[0]
    ref[1, rows, cols] = value[1]


def second_kernel(places, role, before, slots, inverse, out, along_row, along_col):
    step = pl.program_id(0)

    @pl.when(step == 0)
    def _():
        pltpu.sync_copy(before, out)

    add_slots(out, places, slots)
    last = step == GROUP // STEP - 1
    long, short = SIDE // RING, 2 * TILE // RING

    @pl.when(last & (role[0] == 0) & (role[1] == 0))
    def _():
        pivots = [cuts((inverse[p, 0], inverse[p, 1])) for p in range(TS)]
        for p in range(TS - 1):
            uppers = {j: cuts(get(out, *tile_at(p, j))) for j in range(p + 1, TS)}
            for i in range(p + 1, TS):
                factor = complex_dot(cuts(get(out, *tile_at(i, p))), pivots[p])
                put(out, *tile_at(i, p), factor)
                factor = cuts(factor)
                for j in range(p + 1, TS):
                    at = tile_at(i, j)
                    put(out, *at, minus(get(out, *at), complex_dot(factor, uppers[j])))
        lower = [get(out, *tile_at(i, j)) for i, j in ((1, 0), (2, 0), (2, 1))]
        lower = jnp.concatenate([jnp.concatenate(x, 1) for x in lower], 0)
        upper = [
            complex_dot(cuts(get(out, *tile_at(i, j))), pivots[j])
            for i, j in ((0, 1), (0, 2), (1, 2))
        ]
        upper = [jnp.concatenate([x[half] for x in upper], 1) for half in (0, 1)]
        for piece in range(RING):
            store_piece(along_row, piece, lower[piece * long : (piece + 1) * long])
            half, start = divmod(piece * short, TILE)
            store_piece(along_col, piece, upper[half][start : start + short])

    @pl.when(last & (role[0] > 0) & (role[1] == 0))
    def _():
        for p in range(TS):
            pivot = cuts((inverse[p, 0], inverse[p, 1]))
            for i in range(TS):
                at = tile_at(i, p)
                put(out, *at, complex_dot(cuts(get(out, *at)), pivot))
        for piece in range(RING):
            rows = slice(piece * long, (piece + 1) * long)
            store_piece(along_row, piece, jnp.concatenate(get(out, rows, slice(0, TILE)), 1))

    @pl.when(last & (role[0] == 0) & (role[1] > 0))
    def _():
        for piece in range(RING):
            half, start = divmod(piece * short, TILE)
            store_piece(along_col, piece, out[half, start : start + short, :])


def whole(shape):
    return pl.BlockSpec(shape, lambda *_: (0,) * len(shape))


def slot_spec(slots):
    return pl.BlockSpec((STEP,) + slots.shape[1:], lambda s, *_: (s, 0, 0))


ANYWHERE = pl.BlockSpec(memory_space=pl.ANY)
HELD = pl.BlockSpec(memory_space=pltpu.VMEM)
ADD_COST = pl.CostEstimate(
    flops=4 * GROUP * TILE**3, bytes_accessed=20 * 2**20, transcendentals=0
)


def add_first(places, own_places, before, own_left, own_right, slots):
    return pl.pallas_call(
        first_kernel,
        grid_spec=pltpu.PrefetchScalarGridSpec(
            num_scalar_prefetch=2,
            grid=(GROUP // STEP,),
            in_specs=[ANYWHERE, whole(own_left.shape), whole(own_right.shape), slot_spec(slots)],
            out_specs=whole(before.shape),
        ),
        out_shape=jax.ShapeDtypeStruct(before.shape, F32),
        compiler_params=pltpu.CompilerParams(vmem_limit_bytes=VMEM_BYTES),
        cost_estimate=ADD_COST,
    )(places, own_places, before, own_left, own_right, slots)


def row_shape(panels):
    return (RING, SIDE // RING + CODE_ROWS, 2 * TILE * panels)


def col_shape(panels):
    return (RING, 2 * TILE * panels // RING + CODE_ROWS, SIDE)


def coded(shape):
    return jax.ShapeDtypeStruct(shape, jnp.int16)


def add_second(places, role, before, slots, inverse):
    return pl.pallas_call(
        second_kernel,
        grid_spec=pltpu.PrefetchScalarGridSpec(
            num_scalar_prefetch=2,
            grid=(GROUP // STEP,),
            in_specs=[ANYWHERE, slot_spec(slots), whole(inverse.shape)],
            out_specs=[whole(before.shape), whole(row_shape(1)), whole(col_shape(1))],
        ),
        out_shape=[
            jax.ShapeDtypeStruct(before.shape, F32),
            coded(row_shape(1)),
            coded(col_shape(1)),
        ],
        compiler_params=pltpu.CompilerParams(vmem_limit_bytes=VMEM_BYTES),
        cost_estimate=ADD_COST,
    )(places, role, before, slots, inverse)


def unpack(refs, place, high, low):
    rows = refs[0].shape[0] - CODE_ROWS
    for ref, shift in zip(refs, (0, 2, RING - 1, 1)):
        at = ((place + shift) & (RING - 1)) * rows
        h, l = cut(decode(ref[:rows, :], ref[rows:, :]))
        high[pl.ds(pl.multiple_of(at, 16), rows), :] = h
        low[pl.ds(pl.multiple_of(at, 16), rows), :] = l


def trailing(held, rows, left, right):
    panels = left[0].shape[1] // (2 * TILE)

    def turned(x, imag):
        parts = []
        for p in range(panels):
            a = x[rows, 2 * p * TILE : (2 * p + 1) * TILE]
            b = x[rows, (2 * p + 1) * TILE : (2 * p + 2) * TILE]
            parts += [b, a] if imag else [a, -b]
        return jnp.concatenate(parts, 1)

    for half in (0, 1):
        a = [turned(x, half == 1) for x in left]
        for j in range(TS):
            cols = slice(j * TILE, (j + 1) * TILE)
            held[half, rows, cols] -= dot_cut(a, [x[:, cols] for x in right])


def piece_scratch(panels):
    return [pltpu.VMEM((SIDE, 2 * TILE * panels), BF16)] * 2 + [
        pltpu.VMEM((2 * TILE * panels, SIDE), BF16)
    ] * 2


def panel_kernel(role, block, *refs):
    from_row, from_col = refs[:RING], refs[RING : 2 * RING]
    out, along_row, along_col, held, row_high, row_low, col_high, col_low, sem = refs[2 * RING :]

    @pl.when((role[0] > 0) | (role[1] > 0))
    def _():
        fetch = pltpu.make_async_copy(block, held, sem)
        fetch.start()

        @pl.when(role[1] > 0)
        def _():
            unpack(from_row, role[1], row_high, row_low)

        @pl.when(role[0] > 0)
        def _():
            unpack(from_col, role[0], col_high, col_low)

        fetch.wait()

    @pl.when((role[0] > 0) & (role[1] == 0))
    def _():
        def tile(t):
            cols = slice(t * TILE, (t + 1) * TILE)
            return [(col_high[rows, cols], col_low[rows, cols]) for rows in (slice(0, TILE), slice(TILE, 2 * TILE))]

        def chunk(i, carry):
            rows = pl.ds(pl.multiple_of(i * TILE, TILE), TILE)
            cols = [slice(j * TILE, (j + 1) * TILE) for j in range(TS)]
            f0 = cuts(get(held, rows, cols[0]))
            f1 = minus(get(held, rows, cols[1]), complex_dot(f0, tile(0)))
            put(held, rows, cols[1], f1)
            f2 = minus(get(held, rows, cols[2]), complex_dot(f0, tile(1)))
            put(held, rows, cols[2], minus(f2, complex_dot(cuts(f1), tile(2))))
            return carry

        lax.fori_loop(0, TS, chunk, 0)
        store = pltpu.make_async_copy(held, out, sem)
        store.start()
        part = SIDE // RING

        def code_piece(piece, carry):
            rows = pl.ds(pl.multiple_of(piece * part, 8), part)
            wide = [x for j in range(1, TS) for x in get(held, rows, slice(j * TILE, (j + 1) * TILE))]
            store_piece(along_row, piece, jnp.concatenate(wide, 1))
            return carry

        lax.fori_loop(0, RING, code_piece, 0)
        store.wait()

    @pl.when((role[0] == 0) & (role[1] > 0))
    def _():
        def tile(t):
            rows = slice(t * TILE, (t + 1) * TILE)
            return [(row_high[rows, cols], row_low[rows, cols]) for cols in (slice(0, TILE), slice(TILE, 2 * TILE))]

        def chunk(j, carry):
            cols = pl.ds(pl.multiple_of(j * TILE, TILE), TILE)
            rows = [slice(i * TILE, (i + 1) * TILE) for i in range(TS)]
            p0 = cuts(get(held, rows[0], cols))
            p1 = minus(get(held, rows[1], cols), complex_dot(tile(0), p0))
            put(held, rows[1], cols, p1)
            p2 = minus(get(held, rows[2], cols), complex_dot(tile(1), p0))
            put(held, rows[2], cols, minus(p2, complex_dot(tile(2), cuts(p1))))
            return carry

        lax.fori_loop(0, TS, chunk, 0)
        store = pltpu.make_async_copy(held, out, sem)
        store.start()
        for piece in range(RING):
            at, half = divmod(piece, 2)
            store_piece(along_col, piece, held[half, (at + 1) * TILE : (at + 2) * TILE, :])
        store.wait()

    @pl.when((role[0] > 0) & (role[1] > 0))
    def _():
        def chunk(i, carry):
            rows = pl.ds(pl.multiple_of(i * TILE, TILE), TILE)
            trailing(held, rows, (row_high, row_low), (col_high, col_low))
            return carry

        lax.fori_loop(0, TS, chunk, 0)
        pltpu.sync_copy(held, out)


def panel(role, block, from_row, from_col):
    return pl.pallas_call(
        panel_kernel,
        in_specs=[pl.BlockSpec(memory_space=pltpu.SMEM), ANYWHERE] + [HELD] * (2 * RING),
        out_specs=[ANYWHERE, HELD, HELD],
        out_shape=[
            jax.ShapeDtypeStruct(block.shape, F32),
            coded(row_shape(2)),
            coded(col_shape(2)),
        ],
        scratch_shapes=[pltpu.VMEM(block.shape, F32)]
        + piece_scratch(1)
        + [pltpu.SemaphoreType.DMA],
        input_output_aliases={1: 0},
        compiler_params=pltpu.CompilerParams(vmem_limit_bytes=VMEM_BYTES),
    )(role, block, *from_row, *from_col)


def trail_kernel(role, block, *refs):
    from_row, from_col = refs[:RING], refs[RING : 2 * RING]
    out, held, row_high, row_low, col_high, col_low, sem, sems = refs[2 * RING :]

    @pl.when((role[0] > 0) & (role[1] > 0))
    def _():
        fetch = pltpu.make_async_copy(block, held, sem)
        fetch.start()
        unpack(from_row, role[1], row_high, row_low)
        unpack(from_col, role[0], col_high, col_low)
        fetch.wait()

        def store(i):
            rows = pl.ds(pl.multiple_of(i * TILE, TILE), TILE)
            return pltpu.make_async_copy(held.at[:, rows, :], out.at[:, rows, :], sems.at[i])

        def chunk(i, carry):
            rows = pl.ds(pl.multiple_of(i * TILE, TILE), TILE)
            trailing(held, rows, (row_high, row_low), (col_high, col_low))
            store(i).start()
            return carry

        lax.fori_loop(0, TS, chunk, 0)
        for i in range(TS):
            store(i).wait()


def trail(role, block, from_row, from_col):
    return pl.pallas_call(
        trail_kernel,
        in_specs=[pl.BlockSpec(memory_space=pltpu.SMEM), ANYWHERE] + [HELD] * (2 * RING),
        out_specs=ANYWHERE,
        out_shape=jax.ShapeDtypeStruct(block.shape, F32),
        scratch_shapes=[pltpu.VMEM(block.shape, F32)]
        + piece_scratch(2)
        + [pltpu.SemaphoreType.DMA, pltpu.SemaphoreType.DMA((TS,))],
        input_output_aliases={1: 0},
        compiler_params=pltpu.CompilerParams(vmem_limit_bytes=VMEM_BYTES),
    )(role, block, *from_row, *from_col)


def spread(pieces, axis):
    got = [lax.ppermute(pieces[d], axis, [(0, d)]) for d in (2, 1, 3)]
    here = lax.axis_index(axis)
    return jnp.where(
        here == 0,
        pieces[0],
        jnp.where(here == 2, got[0], jnp.where(here == 1, got[1], got[2])),
    )


def exchange(own, axis):
    others = []
    for shift in (2, 1, 3):
        pairs = [(i, (i + shift) % RING) for i in range(RING)]
        others.append(lax.ppermute(own, axis, [p for p in pairs if p[1] != 0]))
    return [own] + others


def body(
    parent_front,
    child_left,
    child_right,
    tile_ranks,
    destination,
    tile_place,
    row_source,
    col_source,
    own_left,
    own_right,
    own_place,
    pivot_inverse,
):
    joined = ("front", "row")
    role = jnp.stack([lax.axis_index("row"), lax.axis_index("col")]).astype(jnp.int32)
    none = 16 * SENT
    numbers = 16 * jnp.arange(SENT, dtype=jnp.int32) + tile_place
    to_each = jnp.where(
        destination[None, :] == jnp.arange(GROUP, dtype=jnp.int32)[:, None],
        numbers[None, :],
        none,
    )
    first_out = jnp.min(to_each, 1)
    second_out = jnp.min(jnp.where(to_each > first_out[:, None], to_each, none), 1)

    rows = row_source[:, None, :]
    cols = col_source[:, None, :]

    def place_of(number):
        return jnp.where(number < none, number & 15, -1)

    def sent(number, notes):
        filled = (number < none).astype(jnp.int32)
        slots = pack(
            (number >> 4) * filled, filled, tile_ranks, notes, child_left, child_right, rows, cols
        )
        return lax.all_to_all(slots, joined, split_axis=0, concat_axis=0, tiled=True)

    second_slots = sent(second_out, [place_of(second_out), place_of(first_out)])
    first_slots = sent(first_out, [])
    places = second_slots[:, TILE + 2 * RANK : TILE + 2 * RANK + 2, 0].astype(jnp.int32)

    block = add_first(places[:, 0], own_place, parent_front[0], own_left, own_right, second_slots)
    block, row_pieces, col_pieces = add_second(
        places[:, 1], role, block, first_slots, pivot_inverse[0]
    )
    from_row, from_col = spread(row_pieces, "col"), spread(col_pieces, "row")
    from_row, from_col = exchange(from_row, "col"), exchange(from_col, "row")
    block, row_pieces, col_pieces = panel(role, block, from_row, from_col)
    from_row, from_col = spread(row_pieces, "col"), spread(col_pieces, "row")
    from_row, from_col = exchange(from_row, "col"), exchange(from_col, "row")
    return trail(role, block, from_row, from_col)[None]


def solution(mesh):
    joined = ("front", "row", "col")
    tiles = P(joined, None, None)
    return jax.shard_map(
        body,
        mesh=mesh,
        in_specs=(
            P("front", None, "row", "col"),
            tiles,
            tiles,
            P(joined),
            P(joined),
            P(joined),
            P(joined, None),
            P(joined, None),
            tiles,
            tiles,
            P(joined),
            P("front", None, None, None, None),
        ),
        out_specs=P("front", None, "row", "col"),
        check_vma=False,
    )
```

```python
import functools
import math

import jax
import jax.numpy as jnp
from jax import lax
from jax.experimental import pallas as pl
from jax.experimental.pallas import tpu as pltpu
from jax.sharding import PartitionSpec as P

TILE = 256
RANK = 128
TS = 3
SIDE = TS * TILE
SENT = 28
GROUP = 32
RING = 4
CODE_ROWS = 16
NOTE_ROWS = 16
LOG_STEP = math.log(2.0) / 32.0
VMEM_BYTES = 32 * 1024 * 1024
MORE_VMEM_BYTES = 45 * 1024 * 1024
ALL_VMEM_BYTES = 60 * 1024 * 1024
DEPTH = 4
BF16 = jnp.bfloat16
F32 = jnp.float32
IN_HBM = pl.BlockSpec(memory_space=pltpu.HBM)
HELD = pl.BlockSpec(memory_space=pltpu.VMEM)
SCALAR = pl.BlockSpec(memory_space=pltpu.SMEM)


def encode(values):
    peak = jnp.maximum(jnp.max(jnp.abs(values), axis=0, keepdims=True), 1e-30)
    code = jnp.ceil(jnp.log(peak * (1.0 / 32700.0)) * (1.0 / LOG_STEP))
    whole = jnp.round(values * jnp.exp(code * -LOG_STEP))
    whole = jnp.clip(whole, -32767.0, 32767.0).astype(jnp.int32)
    code_rows = jnp.broadcast_to(code.astype(jnp.int32), (CODE_ROWS, values.shape[1]))
    return whole.astype(jnp.int16), code_rows.astype(jnp.int16)


def store_piece(ref, values):
    rows = values.shape[0]
    whole, code_rows = encode(values)
    ref[:rows, :] = whole
    ref[rows:, :] = code_rows


def decode(piece_rows, code_rows):
    code = code_rows[:1].astype(jnp.int32).astype(F32)
    return piece_rows.astype(jnp.int32).astype(F32) * jnp.exp(code * LOG_STEP)


def cut(x):
    high = x.astype(BF16)
    return high, (x - high.astype(F32)).astype(BF16)


def dot(a, b):
    return lax.dot_general(a, b, (((1,), (0,)), ((), ())), preferred_element_type=F32)


def dot_cut(a, b):
    return dot(a[0], b[0]) + (dot(a[0], b[1]) + dot(a[1], b[0]))


def cuts(pair):
    return [cut(x) for x in pair]


def complex_dot(a, b):
    return (
        dot_cut(a[0], b[0]) - dot_cut(a[1], b[1]),
        dot_cut(a[0], b[1]) + dot_cut(a[1], b[0]),
    )


def minus(a, b):
    return a[0] - b[0], a[1] - b[1]


def pack_kernel(
    second, destination, place, ranks, left, right, rows, cols, out, *scratch
):
    number, order, lefts, rights, packed, notes, sem_in, sem_out, sem_notes = scratch

    def clear(d, carry):
        number[0, d] = -1
        number[1, d] = -1
        return carry

    lax.fori_loop(0, GROUP, clear, 0)

    def sort(k, count):
        d = destination[k]
        later = (number[0, d] >= 0).astype(jnp.int32)
        number[later, d] = k
        mine = later == second

        @pl.when(mine)
        def _():
            order[count] = k

        return count + mine.astype(jnp.int32)

    count = lax.fori_loop(0, SENT, sort, 0)

    def fetch(p, slot):
        k = order[p]
        return (
            pltpu.make_async_copy(left.at[k], lefts.at[slot], sem_in.at[slot, 0]),
            pltpu.make_async_copy(right.at[k], rights.at[slot], sem_in.at[slot, 1]),
        )

    def store(d, slot):
        target = out.at[d, pl.ds(0, TILE + 2 * RANK)]
        return pltpu.make_async_copy(packed.at[slot], target, sem_out.at[slot])

    for slot in range(DEPTH):

        @pl.when(slot < count)
        def _(slot=slot):
            for copy in fetch(slot, slot):
                copy.start()

    if second:
        line = lax.broadcasted_iota(jnp.int32, (NOTE_ROWS, TILE), 0)

        def note(d, carry):
            def code(which):
                k = number[which, d]
                return jnp.where(k >= 0, place[jnp.maximum(k, 0)], -1)

            lines = jnp.where(line == 0, code(1), code(0))
            notes[d] = lines.astype(F32).astype(BF16)
            return carry

        lax.fori_loop(0, GROUP, note, 0)
        tell = pltpu.make_async_copy(
            notes, out.at[:, pl.ds(TILE + 2 * RANK, NOTE_ROWS)], sem_notes
        )
        tell.start()

    index = lax.broadcasted_iota(jnp.int32, (TILE, TILE), 0)
    width = lax.broadcasted_iota(jnp.int32, (TILE, 2 * RANK), 1)
    width = jnp.where(width >= RANK, width - RANK, width)
    turned = (((0,), (0,)), ((), ()))

    def onehot(chosen):
        return jnp.where(index == chosen, 1.0, 0.0).astype(BF16)

    def work(p, carry):
        slot = p & (DEPTH - 1)
        k = order[p]
        for copy in fetch(p, slot):
            copy.wait()

        @pl.when(p >= DEPTH)
        def _():
            store(0, slot).wait()

        moved = lax.dot_general(
            onehot(rows[pl.ds(k, 1), :]), lefts[slot], turned, preferred_element_type=F32
        )
        packed[slot, :TILE, :] = jnp.where(width < ranks[k], moved, 0.0).astype(BF16)
        packed[slot, TILE:, :] = lax.dot_general(
            rights[slot], onehot(cols[pl.ds(k, 1), :]), turned, preferred_element_type=F32
        ).astype(BF16)
        store(destination[k], slot).start()

        @pl.when(p + DEPTH < count)
        def _():
            for copy in fetch(p + DEPTH, slot):
                copy.start()

        return carry

    lax.fori_loop(0, count, work, 0)
    for slot in range(DEPTH):

        @pl.when(slot < count)
        def _(slot=slot):
            store(0, slot).wait()

    if second:
        tell.wait()


def pack(second, destination, place, ranks, left, right, rows, cols):
    depth = TILE + 2 * RANK + (NOTE_ROWS if second else 0)
    tiles = pltpu.VMEM((DEPTH, TILE, 2 * RANK), BF16)
    return pl.pallas_call(
        functools.partial(pack_kernel, second),
        in_specs=[SCALAR] * 3 + [IN_HBM] * 2 + [HELD] * 2,
        out_specs=IN_HBM,
        out_shape=jax.ShapeDtypeStruct((GROUP, depth, TILE), BF16),
        scratch_shapes=[
            pltpu.SMEM((2, GROUP), jnp.int32),
            pltpu.SMEM((SENT,), jnp.int32),
            tiles,
            tiles,
            pltpu.VMEM((DEPTH, TILE + 2 * RANK, TILE), BF16),
            pltpu.VMEM((GROUP, NOTE_ROWS, TILE), BF16),
            pltpu.SemaphoreType.DMA((DEPTH, 2)),
            pltpu.SemaphoreType.DMA((DEPTH,)),
            pltpu.SemaphoreType.DMA,
        ],
        compiler_params=pltpu.CompilerParams(vmem_limit_bytes=ALL_VMEM_BYTES),
        cost_estimate=pl.CostEstimate(
            flops=4 * SENT * TILE**3, bytes_accessed=16 * 2**20, transcendentals=0
        ),
    )(destination, place, ranks, left, right, rows, cols)


def add_at(out, place, real, imag):
    a = place // TS
    rows = pl.ds(pl.multiple_of(a * TILE, TILE), TILE)
    cols = pl.ds(pl.multiple_of((place - a * TS) * TILE, TILE), TILE)
    out[0, rows, cols] += real
    out[1, rows, cols] += imag


def add_own(out, place, left, right):
    real_side = jnp.concatenate([right[:, :RANK], -right[:, RANK:]], 1)
    imag_side = jnp.concatenate([right[:, RANK:], right[:, :RANK]], 1)
    contract = (((1,), (1,)), ((), ()))
    add_at(
        out,
        place,
        lax.dot_general(left, real_side, contract, preferred_element_type=F32),
        lax.dot_general(left, imag_side, contract, preferred_element_type=F32),
    )


def add_slots(out, places, slots, scratch, prepare):
    order, arrived, sems = scratch

    def sort(slot, count):
        mine = places[slot] >= 0

        @pl.when(mine)
        def _():
            order[count] = slot

        return count + mine.astype(jnp.int32)

    count = lax.fori_loop(0, GROUP, sort, 0)

    def fetch(p, held):
        source = slots.at[order[p], pl.ds(0, TILE + 2 * RANK)]
        return pltpu.make_async_copy(source, arrived.at[held], sems.at[held])

    for p in range(DEPTH):

        @pl.when(p < count)
        def _(p=p):
            fetch(p, p).start()

    prepare()

    def work(p, carry):
        held = p & (DEPTH - 1)
        fetch(p, held).wait()
        left = arrived[held, :TILE, :]
        top = arrived[held, TILE : TILE + RANK, :]
        bottom = arrived[held, TILE + RANK :, :]
        add_at(
            out,
            places[order[p]],
            dot(left, jnp.concatenate([top, -bottom], 0)),
            dot(left, jnp.concatenate([bottom, top], 0)),
        )

        @pl.when(p + DEPTH < count)
        def _():
            fetch(p + DEPTH, held).start()

        return carry

    lax.fori_loop(0, count, work, 0)


def add_scratch():
    return [
        pltpu.SMEM((GROUP,), jnp.int32),
        pltpu.VMEM((DEPTH, TILE + 2 * RANK, TILE), BF16),
        pltpu.SemaphoreType.DMA((DEPTH,)),
    ]


def first_kernel(places, own_places, before, own_left, own_right, slots, out, *scratch):
    def prepare():
        pltpu.sync_copy(before, out)

        def own_step(j, carry):
            add_own(out, own_places[j], own_left[j], own_right[j])
            return carry

        lax.fori_loop(0, own_left.shape[0], own_step, 0)

    add_slots(out, places, slots, scratch, prepare)


def tile_at(i, j):
    return slice(i * TILE, (i + 1) * TILE), slice(j * TILE, (j + 1) * TILE)


def get(ref, rows, cols):
    return ref[0, rows, cols], ref[1, rows, cols]


def put(ref, rows, cols, value):
    ref[0, rows, cols] = value[0]
    ref[1, rows, cols] = value[1]


def second_kernel(places, role, before, slots, inverse, out, *refs):
    along_row, along_col = refs[:RING], refs[RING : 2 * RING]

    def prepare():
        out[...] = before[...]

    add_slots(out, places, slots, refs[2 * RING :], prepare)
    long, short = SIDE // RING, 2 * TILE // RING

    @pl.when((role[0] == 0) & (role[1] == 0))
    def _():
        pivots = [cuts((inverse[p, 0], inverse[p, 1])) for p in range(TS)]
        for p in range(TS - 1):
            uppers = {j: cuts(get(out, *tile_at(p, j))) for j in range(p + 1, TS)}
            for i in range(p + 1, TS):
                factor = complex_dot(cuts(get(out, *tile_at(i, p))), pivots[p])
                put(out, *tile_at(i, p), factor)
                factor = cuts(factor)
                for j in range(p + 1, TS):
                    at = tile_at(i, j)
                    put(out, *at, minus(get(out, *at), complex_dot(factor, uppers[j])))
        lower = [get(out, *tile_at(i, j)) for i, j in ((1, 0), (2, 0), (2, 1))]
        lower = jnp.concatenate([jnp.concatenate(x, 1) for x in lower], 0)
        upper = [
            complex_dot(cuts(get(out, *tile_at(i, j))), pivots[j])
            for i, j in ((0, 1), (0, 2), (1, 2))
        ]
        upper = [jnp.concatenate([x[half] for x in upper], 1) for half in (0, 1)]
        for piece in range(RING):
            store_piece(along_row[piece], lower[piece * long : (piece + 1) * long])
            half, start = divmod(piece * short, TILE)
            store_piece(along_col[piece], upper[half][start : start + short])

    @pl.when((role[0] > 0) & (role[1] == 0))
    def _():
        for p in range(TS):
            pivot = cuts((inverse[p, 0], inverse[p, 1]))
            for i in range(TS):
                at = tile_at(i, p)
                put(out, *at, complex_dot(cuts(get(out, *at)), pivot))
        for piece in range(RING):
            rows = slice(piece * long, (piece + 1) * long)
            store_piece(along_row[piece], jnp.concatenate(get(out, rows, slice(0, TILE)), 1))

    @pl.when((role[0] == 0) & (role[1] > 0))
    def _():
        for piece in range(RING):
            half, start = divmod(piece * short, TILE)
            store_piece(along_col[piece], out[half, start : start + short, :])


ADD_COST = pl.CostEstimate(
    flops=4 * GROUP * TILE**3, bytes_accessed=20 * 2**20, transcendentals=0
)


def add_first(places, own_places, before, own_left, own_right, slots):
    return pl.pallas_call(
        first_kernel,
        in_specs=[SCALAR, SCALAR, IN_HBM, HELD, HELD, IN_HBM],
        out_specs=HELD,
        out_shape=jax.ShapeDtypeStruct(before.shape, F32),
        scratch_shapes=add_scratch(),
        compiler_params=pltpu.CompilerParams(vmem_limit_bytes=MORE_VMEM_BYTES),
        cost_estimate=ADD_COST,
    )(places, own_places, before, own_left, own_right, slots)


def row_shape(panels):
    return (SIDE // RING + CODE_ROWS, 2 * TILE * panels)


def col_shape(panels):
    return (2 * TILE * panels // RING + CODE_ROWS, SIDE)


def coded(shape):
    return jax.ShapeDtypeStruct(shape, jnp.int16)


def pieces_of(panels):
    return [coded(row_shape(panels))] * RING + [coded(col_shape(panels))] * RING


def add_second(places, role, before, slots, inverse):
    return pl.pallas_call(
        second_kernel,
        in_specs=[SCALAR, SCALAR, HELD, IN_HBM, HELD],
        out_specs=[HELD] * (1 + 2 * RING),
        out_shape=[jax.ShapeDtypeStruct(before.shape, F32)] + pieces_of(1),
        scratch_shapes=add_scratch(),
        compiler_params=pltpu.CompilerParams(vmem_limit_bytes=MORE_VMEM_BYTES),
        cost_estimate=ADD_COST,
    )(places, role, before, slots, inverse)


def unpack(refs, place, high, low):
    rows = refs[0].shape[0] - CODE_ROWS
    for ref, shift in zip(refs, (0, 2, RING - 1, 1)):
        at = ((place + shift) & (RING - 1)) * rows
        h, l = cut(decode(ref[:rows, :], ref[rows:, :]))
        high[pl.ds(pl.multiple_of(at, 16), rows), :] = h
        low[pl.ds(pl.multiple_of(at, 16), rows), :] = l


def trailing(block, out, rows, left, right):
    panels = left[0].shape[1] // (2 * TILE)

    def turned(x, imag):
        parts = []
        for p in range(panels):
            a = x[rows, 2 * p * TILE : (2 * p + 1) * TILE]
            b = x[rows, (2 * p + 1) * TILE : (2 * p + 2) * TILE]
            parts += [b, a] if imag else [a, -b]
        return jnp.concatenate(parts, 1)

    for half in (0, 1):
        a = [turned(x, half == 1) for x in left]
        for j in range(TS):
            cols = slice(j * TILE, (j + 1) * TILE)
            product = dot_cut(a, [x[:, cols] for x in right])
            out[half, rows, cols] = block[half, rows, cols] - product


def piece_scratch(panels):
    return [pltpu.VMEM((SIDE, 2 * TILE * panels), BF16)] * 2 + [
        pltpu.VMEM((2 * TILE * panels, SIDE), BF16)
    ] * 2


def panel_kernel(role, block, *refs):
    from_row, from_col = refs[:RING], refs[RING : 2 * RING]
    out, along_row, along_col = (
        refs[2 * RING],
        refs[2 * RING + 1 : 3 * RING + 1],
        refs[3 * RING + 1 : 4 * RING + 1],
    )
    row_high, row_low, col_high, col_low = refs[4 * RING + 1 :]
    parts = [slice(t * TILE, (t + 1) * TILE) for t in range(TS)]

    @pl.when(role[1] > 0)
    def _():
        unpack(from_row, role[1], row_high, row_low)

    @pl.when(role[0] > 0)
    def _():
        unpack(from_col, role[0], col_high, col_low)

    @pl.when((role[0] == 0) & (role[1] == 0))
    def _():
        out[...] = block[...]

    @pl.when((role[0] > 0) & (role[1] == 0))
    def _():
        def tile(t):
            return [(col_high[rows, parts[t]], col_low[rows, parts[t]]) for rows in parts[:2]]

        def chunk(i, carry):
            rows = pl.ds(pl.multiple_of(i * TILE, TILE), TILE)
            f0 = get(block, rows, parts[0])
            put(out, rows, parts[0], f0)
            f0 = cuts(f0)
            f1 = minus(get(block, rows, parts[1]), complex_dot(f0, tile(0)))
            put(out, rows, parts[1], f1)
            f2 = minus(get(block, rows, parts[2]), complex_dot(f0, tile(1)))
            put(out, rows, parts[2], minus(f2, complex_dot(cuts(f1), tile(2))))
            return carry

        lax.fori_loop(0, TS, chunk, 0)
        part = SIDE // RING
        for piece in range(RING):
            rows = slice(piece * part, (piece + 1) * part)
            wide = [x for cols in parts[1:] for x in get(out, rows, cols)]
            store_piece(along_row[piece], jnp.concatenate(wide, 1))

    @pl.when((role[0] == 0) & (role[1] > 0))
    def _():
        def tile(t):
            return [(row_high[parts[t], cols], row_low[parts[t], cols]) for cols in parts[:2]]

        def chunk(j, carry):
            cols = pl.ds(pl.multiple_of(j * TILE, TILE), TILE)
            p0 = get(block, parts[0], cols)
            put(out, parts[0], cols, p0)
            p0 = cuts(p0)
            p1 = minus(get(block, parts[1], cols), complex_dot(tile(0), p0))
            put(out, parts[1], cols, p1)
            p2 = minus(get(block, parts[2], cols), complex_dot(tile(1), p0))
            put(out, parts[2], cols, minus(p2, complex_dot(tile(2), cuts(p1))))
            return carry

        lax.fori_loop(0, TS, chunk, 0)
        for piece in range(RING):
            at, half = divmod(piece, 2)
            store_piece(along_col[piece], out[half, parts[at + 1], :])

    @pl.when((role[0] > 0) & (role[1] > 0))
    def _():
        def chunk(i, carry):
            rows = pl.ds(pl.multiple_of(i * TILE, TILE), TILE)
            trailing(block, out, rows, (row_high, row_low), (col_high, col_low))
            return carry

        lax.fori_loop(0, TS, chunk, 0)


def panel(role, block, from_row, from_col):
    return pl.pallas_call(
        panel_kernel,
        in_specs=[SCALAR] + [HELD] * (1 + 2 * RING),
        out_specs=[HELD] * (1 + 2 * RING),
        out_shape=[jax.ShapeDtypeStruct(block.shape, F32)] + pieces_of(2),
        scratch_shapes=piece_scratch(1),
        compiler_params=pltpu.CompilerParams(vmem_limit_bytes=VMEM_BYTES),
    )(role, block, *from_row, *from_col)


def trail_kernel(role, block, *refs):
    from_row, from_col = refs[:RING], refs[RING : 2 * RING]
    out, held, row_high, row_low, col_high, col_low, sem, sems = refs[2 * RING :]
    inner = (role[0] > 0) & (role[1] > 0)

    @pl.when(jnp.logical_not(inner))
    def _():
        store = pltpu.make_async_copy(block, out, sem)
        store.start()
        store.wait()

    @pl.when(inner)
    def _():
        unpack(from_row, role[1], row_high, row_low)
        unpack(from_col, role[0], col_high, col_low)

        def store(i):
            rows = pl.ds(pl.multiple_of(i * TILE, TILE), TILE)
            return pltpu.make_async_copy(held.at[:, rows, :], out.at[:, rows, :], sems.at[i])

        def chunk(i, carry):
            rows = pl.ds(pl.multiple_of(i * TILE, TILE), TILE)
            trailing(block, held, rows, (row_high, row_low), (col_high, col_low))
            store(i).start()
            return carry

        lax.fori_loop(0, TS, chunk, 0)
        for i in range(TS):
            store(i).wait()


def trail(role, block, from_row, from_col):
    return pl.pallas_call(
        trail_kernel,
        in_specs=[SCALAR] + [HELD] * (1 + 2 * RING),
        out_specs=IN_HBM,
        out_shape=jax.ShapeDtypeStruct(block.shape, F32),
        scratch_shapes=[pltpu.VMEM(block.shape, F32)]
        + piece_scratch(2)
        + [pltpu.SemaphoreType.DMA, pltpu.SemaphoreType.DMA((TS,))],
        compiler_params=pltpu.CompilerParams(vmem_limit_bytes=VMEM_BYTES),
    )(role, block, *from_row, *from_col)


def spread(pieces, axis):
    got = [lax.ppermute(pieces[d], axis, [(0, d)]) for d in (2, 1, 3)]
    here = lax.axis_index(axis)
    return jnp.where(
        here == 0,
        pieces[0],
        jnp.where(here == 2, got[0], jnp.where(here == 1, got[1], got[2])),
    )


def exchange(own, axis):
    others = []
    for shift in (2, 1, 3):
        pairs = [(i, (i + shift) % RING) for i in range(RING)]
        others.append(lax.ppermute(own, axis, [p for p in pairs if p[1] != 0]))
    return [own] + others


def body(
    parent_front,
    child_left,
    child_right,
    tile_ranks,
    destination,
    tile_place,
    row_source,
    col_source,
    own_left,
    own_right,
    own_place,
    pivot_inverse,
):
    joined = ("front", "row")
    role = jnp.stack([lax.axis_index("row"), lax.axis_index("col")]).astype(jnp.int32)

    def sent(second):
        slots = pack(
            second,
            destination,
            tile_place,
            tile_ranks,
            child_left,
            child_right,
            row_source,
            col_source,
        )
        return lax.all_to_all(slots, joined, split_axis=0, concat_axis=0, tiled=True)

    second_slots = sent(1)
    first_slots = sent(0)
    places = second_slots[:, TILE + 2 * RANK : TILE + 2 * RANK + 2, 0].astype(jnp.int32)

    block = add_first(places[:, 0], own_place, parent_front[0], own_left, own_right, second_slots)
    block, *pieces = add_second(places[:, 1], role, block, first_slots, pivot_inverse[0])
    from_row, from_col = spread(pieces[:RING], "col"), spread(pieces[RING:], "row")
    from_row, from_col = exchange(from_row, "col"), exchange(from_col, "row")
    block, *pieces = panel(role, block, from_row, from_col)
    from_row, from_col = spread(pieces[:RING], "col"), spread(pieces[RING:], "row")
    from_row, from_col = exchange(from_row, "col"), exchange(from_col, "row")
    return trail(role, block, from_row, from_col)[None]


def solution(mesh):
    joined = ("front", "row", "col")
    tiles = P(joined, None, None)
    return jax.shard_map(
        body,
        mesh=mesh,
        in_specs=(
            P("front", None, "row", "col"),
            tiles,
            tiles,
            P(joined),
            P(joined),
            P(joined),
            P(joined, None),
            P(joined, None),
            tiles,
            tiles,
            P(joined),
            P("front", None, None, None, None),
        ),
        out_specs=P("front", None, "row", "col"),
        check_vma=False,
    )
```

```python
import functools
import math

import jax
import jax.numpy as jnp
from jax import lax
from jax.experimental import pallas as pl
from jax.experimental.pallas import tpu as pltpu
from jax.sharding import PartitionSpec as P

TILE = 256
RANK = 128
TS = 3
SIDE = TS * TILE
SENT = 28
GROUP = 32
HALVES = 2
ARRIVALS = 4
CHUNK = 64
CODE_ROWS = 16
NOTE_ROWS = 16
LOG_STEP = math.log(2.0) / 32.0
VMEM_BYTES = 32 * 1024 * 1024
MORE_VMEM_BYTES = 45 * 1024 * 1024
ALL_VMEM_BYTES = 60 * 1024 * 1024
DEPTH = 4
BF16 = jnp.bfloat16
F32 = jnp.float32
IN_HBM = pl.BlockSpec(memory_space=pltpu.HBM)
HELD = pl.BlockSpec(memory_space=pltpu.VMEM)
SCALAR = pl.BlockSpec(memory_space=pltpu.SMEM)


def encode(values):
    peak = jnp.maximum(jnp.max(jnp.abs(values), axis=0, keepdims=True), 1e-30)
    code = jnp.ceil(jnp.log(peak * (1.0 / 32700.0)) * (1.0 / LOG_STEP))
    whole = jnp.round(values * jnp.exp(code * -LOG_STEP))
    whole = jnp.clip(whole, -32767.0, 32767.0).astype(jnp.int32)
    code_rows = jnp.broadcast_to(code.astype(jnp.int32), (CODE_ROWS, values.shape[1]))
    return whole.astype(jnp.int16), code_rows.astype(jnp.int16)


def store_piece(ref, values):
    rows = values.shape[0]
    whole, code_rows = encode(values)
    ref[:rows, :] = whole
    ref[rows:, :] = code_rows


def cut(x):
    high = x.astype(BF16)
    return high, (x - high.astype(F32)).astype(BF16)


def dot(a, b):
    return lax.dot_general(a, b, (((1,), (0,)), ((), ())), preferred_element_type=F32)


def dot_cut(a, b):
    return dot(a[0], b[0]) + (dot(a[0], b[1]) + dot(a[1], b[0]))


def cuts(pair):
    return [cut(x) for x in pair]


def complex_dot(a, b):
    return (
        dot_cut(a[0], b[0]) - dot_cut(a[1], b[1]),
        dot_cut(a[0], b[1]) + dot_cut(a[1], b[0]),
    )


def minus(a, b):
    return a[0] - b[0], a[1] - b[1]


def pack_kernel(
    second, destination, place, ranks, left, right, rows, cols, out, *scratch
):
    number, order, lefts, rights, packed, notes, sem_in, sem_out, sem_notes = scratch

    def clear(d, carry):
        number[0, d] = -1
        number[1, d] = -1
        return carry

    lax.fori_loop(0, GROUP, clear, 0)

    def sort(k, count):
        d = destination[k]
        later = (number[0, d] >= 0).astype(jnp.int32)
        number[later, d] = k
        mine = later == second

        @pl.when(mine)
        def _():
            order[count] = k

        return count + mine.astype(jnp.int32)

    count = lax.fori_loop(0, SENT, sort, 0)

    def fetch(p, slot):
        k = order[p]
        return (
            pltpu.make_async_copy(left.at[k], lefts.at[slot], sem_in.at[slot, 0]),
            pltpu.make_async_copy(right.at[k], rights.at[slot], sem_in.at[slot, 1]),
        )

    def store(d, slot):
        target = out.at[d, pl.ds(0, TILE + 2 * RANK)]
        return pltpu.make_async_copy(packed.at[slot], target, sem_out.at[slot])

    for slot in range(DEPTH):

        @pl.when(slot < count)
        def _(slot=slot):
            for copy in fetch(slot, slot):
                copy.start()

    if second:
        line = lax.broadcasted_iota(jnp.int32, (NOTE_ROWS, TILE), 0)

        def note(d, carry):
            def code(which):
                k = number[which, d]
                return jnp.where(k >= 0, place[jnp.maximum(k, 0)], -1)

            lines = jnp.where(line == 0, code(1), code(0))
            notes[d] = lines.astype(F32).astype(BF16)
            return carry

        lax.fori_loop(0, GROUP, note, 0)
        tell = pltpu.make_async_copy(
            notes, out.at[:, pl.ds(TILE + 2 * RANK, NOTE_ROWS)], sem_notes
        )
        tell.start()

    index = lax.broadcasted_iota(jnp.int32, (TILE, TILE), 0)
    width = lax.broadcasted_iota(jnp.int32, (TILE, 2 * RANK), 1)
    width = jnp.where(width >= RANK, width - RANK, width)
    turned = (((0,), (0,)), ((), ()))

    def onehot(chosen):
        return jnp.where(index == chosen, 1.0, 0.0).astype(BF16)

    def work(p, carry):
        slot = p & (DEPTH - 1)
        k = order[p]
        for copy in fetch(p, slot):
            copy.wait()

        @pl.when(p >= DEPTH)
        def _():
            store(0, slot).wait()

        moved = lax.dot_general(
            onehot(rows[pl.ds(k, 1), :]), lefts[slot], turned, preferred_element_type=F32
        )
        packed[slot, :TILE, :] = jnp.where(width < ranks[k], moved, 0.0).astype(BF16)
        packed[slot, TILE:, :] = lax.dot_general(
            rights[slot], onehot(cols[pl.ds(k, 1), :]), turned, preferred_element_type=F32
        ).astype(BF16)
        store(destination[k], slot).start()

        @pl.when(p + DEPTH < count)
        def _():
            for copy in fetch(p + DEPTH, slot):
                copy.start()

        return carry

    lax.fori_loop(0, count, work, 0)
    for slot in range(DEPTH):

        @pl.when(slot < count)
        def _(slot=slot):
            store(0, slot).wait()

    if second:
        tell.wait()


def pack(second, destination, place, ranks, left, right, rows, cols):
    depth = TILE + 2 * RANK + (NOTE_ROWS if second else 0)
    tiles = pltpu.VMEM((DEPTH, TILE, 2 * RANK), BF16)
    return pl.pallas_call(
        functools.partial(pack_kernel, second),
        in_specs=[SCALAR] * 3 + [IN_HBM] * 2 + [HELD] * 2,
        out_specs=IN_HBM,
        out_shape=jax.ShapeDtypeStruct((GROUP, depth, TILE), BF16),
        scratch_shapes=[
            pltpu.SMEM((2, GROUP), jnp.int32),
            pltpu.SMEM((SENT,), jnp.int32),
            tiles,
            tiles,
            pltpu.VMEM((DEPTH, TILE + 2 * RANK, TILE), BF16),
            pltpu.VMEM((GROUP, NOTE_ROWS, TILE), BF16),
            pltpu.SemaphoreType.DMA((DEPTH, 2)),
            pltpu.SemaphoreType.DMA((DEPTH,)),
            pltpu.SemaphoreType.DMA,
        ],
        compiler_params=pltpu.CompilerParams(vmem_limit_bytes=ALL_VMEM_BYTES),
        cost_estimate=pl.CostEstimate(
            flops=4 * SENT * TILE**3, bytes_accessed=16 * 2**20, transcendentals=0
        ),
    )(destination, place, ranks, left, right, rows, cols)


def add_at(out, place, real, imag):
    a = place // TS
    rows = pl.ds(pl.multiple_of(a * TILE, TILE), TILE)
    cols = pl.ds(pl.multiple_of((place - a * TS) * TILE, TILE), TILE)
    out[0, rows, cols] += real
    out[1, rows, cols] += imag


def add_own(out, place, left, right):
    real_side = jnp.concatenate([right[:, :RANK], -right[:, RANK:]], 1)
    imag_side = jnp.concatenate([right[:, RANK:], right[:, :RANK]], 1)
    contract = (((1,), (1,)), ((), ()))
    add_at(
        out,
        place,
        lax.dot_general(left, real_side, contract, preferred_element_type=F32),
        lax.dot_general(left, imag_side, contract, preferred_element_type=F32),
    )


def add_slots(out, places, slots, scratch, prepare):
    order, arrived, sems = scratch

    def sort(slot, count):
        mine = places[slot] >= 0

        @pl.when(mine)
        def _():
            order[count] = slot

        return count + mine.astype(jnp.int32)

    count = lax.fori_loop(0, GROUP, sort, 0)

    def fetch(p, held):
        source = slots.at[order[p], pl.ds(0, TILE + 2 * RANK)]
        return pltpu.make_async_copy(source, arrived.at[held], sems.at[held])

    for p in range(DEPTH):

        @pl.when(p < count)
        def _(p=p):
            fetch(p, p).start()

    prepare()

    def work(p, carry):
        held = p & (DEPTH - 1)
        fetch(p, held).wait()
        left = arrived[held, :TILE, :]
        top = arrived[held, TILE : TILE + RANK, :]
        bottom = arrived[held, TILE + RANK :, :]
        add_at(
            out,
            places[order[p]],
            dot(left, jnp.concatenate([top, -bottom], 0)),
            dot(left, jnp.concatenate([bottom, top], 0)),
        )

        @pl.when(p + DEPTH < count)
        def _():
            fetch(p + DEPTH, held).start()

        return carry

    lax.fori_loop(0, count, work, 0)


def add_scratch():
    return [
        pltpu.SMEM((GROUP,), jnp.int32),
        pltpu.VMEM((DEPTH, TILE + 2 * RANK, TILE), BF16),
        pltpu.SemaphoreType.DMA((DEPTH,)),
    ]


def first_kernel(places, own_places, before, own_left, own_right, slots, out, *scratch):
    def prepare():
        pltpu.sync_copy(before, out)

        def own_step(j, carry):
            add_own(out, own_places[j], own_left[j], own_right[j])
            return carry

        lax.fori_loop(0, own_left.shape[0], own_step, 0)

    add_slots(out, places, slots, scratch, prepare)


def tile_at(i, j):
    return slice(i * TILE, (i + 1) * TILE), slice(j * TILE, (j + 1) * TILE)


def get(ref, rows, cols):
    return ref[0, rows, cols], ref[1, rows, cols]


def put(ref, rows, cols, value):
    ref[0, rows, cols] = value[0]
    ref[1, rows, cols] = value[1]


def second_kernel(places, role, before, slots, inverse, out, *refs):
    along_row, along_col = refs[:HALVES], refs[HALVES : 2 * HALVES]

    def prepare():
        out[...] = before[...]

    add_slots(out, places, slots, refs[2 * HALVES :], prepare)
    long = SIDE // HALVES

    @pl.when((role[0] == 0) & (role[1] == 0))
    def _():
        pivots = [cuts((inverse[p, 0], inverse[p, 1])) for p in range(TS)]
        for p in range(TS - 1):
            uppers = {j: cuts(get(out, *tile_at(p, j))) for j in range(p + 1, TS)}
            for i in range(p + 1, TS):
                factor = complex_dot(cuts(get(out, *tile_at(i, p))), pivots[p])
                put(out, *tile_at(i, p), factor)
                factor = cuts(factor)
                for j in range(p + 1, TS):
                    at = tile_at(i, j)
                    put(out, *at, minus(get(out, *at), complex_dot(factor, uppers[j])))
        lower = [get(out, *tile_at(i, j)) for i, j in ((1, 0), (2, 0), (2, 1))]
        lower = jnp.concatenate([jnp.concatenate(x, 1) for x in lower], 0)
        upper = [
            complex_dot(cuts(get(out, *tile_at(i, j))), pivots[j])
            for i, j in ((0, 1), (0, 2), (1, 2))
        ]
        upper = [jnp.concatenate([x[half] for x in upper], 1) for half in (0, 1)]
        for half in range(HALVES):
            store_piece(along_row[half], lower[half * long : (half + 1) * long])
            store_piece(along_col[half], upper[half])

    @pl.when((role[0] > 0) & (role[1] == 0))
    def _():
        for p in range(TS):
            pivot = cuts((inverse[p, 0], inverse[p, 1]))
            for i in range(TS):
                at = tile_at(i, p)
                put(out, *at, complex_dot(cuts(get(out, *at)), pivot))
        for half in range(HALVES):
            rows = slice(half * long, (half + 1) * long)
            store_piece(along_row[half], jnp.concatenate(get(out, rows, slice(0, TILE)), 1))

    @pl.when((role[0] == 0) & (role[1] > 0))
    def _():
        for half in range(HALVES):
            store_piece(along_col[half], out[half, :TILE, :])


ADD_COST = pl.CostEstimate(
    flops=4 * GROUP * TILE**3, bytes_accessed=20 * 2**20, transcendentals=0
)


def add_first(places, own_places, before, own_left, own_right, slots):
    return pl.pallas_call(
        first_kernel,
        in_specs=[SCALAR, SCALAR, IN_HBM, HELD, HELD, IN_HBM],
        out_specs=HELD,
        out_shape=jax.ShapeDtypeStruct(before.shape, F32),
        scratch_shapes=add_scratch(),
        compiler_params=pltpu.CompilerParams(vmem_limit_bytes=MORE_VMEM_BYTES),
        cost_estimate=ADD_COST,
    )(places, own_places, before, own_left, own_right, slots)


def row_shape(panels):
    return (SIDE // HALVES + CODE_ROWS, 2 * TILE * panels)


def col_shape(panels):
    return (2 * TILE * panels // HALVES + CODE_ROWS, SIDE)


def coded(shape):
    return jax.ShapeDtypeStruct(shape, jnp.int16)


def pieces_of(panels):
    return [coded(row_shape(panels))] * HALVES + [coded(col_shape(panels))] * HALVES


def add_second(places, role, before, slots, inverse):
    return pl.pallas_call(
        second_kernel,
        in_specs=[SCALAR, SCALAR, HELD, IN_HBM, HELD],
        out_specs=[HELD] * (1 + 2 * HALVES),
        out_shape=[jax.ShapeDtypeStruct(before.shape, F32)] + pieces_of(1),
        scratch_shapes=add_scratch(),
        compiler_params=pltpu.CompilerParams(vmem_limit_bytes=MORE_VMEM_BYTES),
        cost_estimate=ADD_COST,
    )(places, role, before, slots, inverse)


def unpack(refs, place, high, low):
    one, three, plus, minus = refs
    half = one.shape[0] - CODE_ROWS
    scales = lambda ref: jnp.exp(ref[half:, :][:1].astype(jnp.int32).astype(F32) * LOG_STEP)

    for at, pair in ((1, (one, plus)), (2, (plus, minus)), (3, (minus, three))):

        @pl.when(place == at)
        def _(pair=pair):
            for which, ref in enumerate(pair):
                scale = scales(ref)

                def chunk(i, carry, ref=ref, scale=scale, which=which):
                    rows = pl.ds(pl.multiple_of(i * CHUNK, CHUNK), CHUNK)
                    into = pl.ds(pl.multiple_of(which * half + i * CHUNK, CHUNK), CHUNK)
                    values = ref[rows, :].astype(jnp.int32).astype(F32) * scale
                    high[into, :], low[into, :] = cut(values)
                    return carry

                lax.fori_loop(0, half // CHUNK, chunk, 0)


def trailing(block, out, rows, left, right):
    panels = left[0].shape[1] // (2 * TILE)

    def turned(x, imag):
        parts = []
        for p in range(panels):
            a = x[rows, 2 * p * TILE : (2 * p + 1) * TILE]
            b = x[rows, (2 * p + 1) * TILE : (2 * p + 2) * TILE]
            parts += [b, a] if imag else [a, -b]
        return jnp.concatenate(parts, 1)

    for half in (0, 1):
        a = [turned(x, half == 1) for x in left]
        for j in range(TS):
            cols = slice(j * TILE, (j + 1) * TILE)
            product = dot_cut(a, [x[:, cols] for x in right])
            out[half, rows, cols] = block[half, rows, cols] - product


def piece_scratch(panels):
    return [pltpu.VMEM((SIDE, 2 * TILE * panels), BF16)] * 2 + [
        pltpu.VMEM((2 * TILE * panels, SIDE), BF16)
    ] * 2


def panel_kernel(role, block, *refs):
    from_row, from_col = refs[:ARRIVALS], refs[ARRIVALS : 2 * ARRIVALS]
    out, *refs = refs[2 * ARRIVALS :]
    along_row, along_col = refs[:HALVES], refs[HALVES : 2 * HALVES]
    row_high, row_low, col_high, col_low = refs[2 * HALVES :]
    parts = [slice(t * TILE, (t + 1) * TILE) for t in range(TS)]

    @pl.when(role[1] > 0)
    def _():
        unpack(from_row, role[1], row_high, row_low)

    @pl.when(role[0] > 0)
    def _():
        unpack(from_col, role[0], col_high, col_low)

    @pl.when((role[0] == 0) & (role[1] == 0))
    def _():
        out[...] = block[...]

    @pl.when((role[0] > 0) & (role[1] == 0))
    def _():
        def tile(t):
            return [(col_high[rows, parts[t]], col_low[rows, parts[t]]) for rows in parts[:2]]

        def chunk(i, carry):
            rows = pl.ds(pl.multiple_of(i * TILE, TILE), TILE)
            f0 = get(block, rows, parts[0])
            put(out, rows, parts[0], f0)
            f0 = cuts(f0)
            f1 = minus(get(block, rows, parts[1]), complex_dot(f0, tile(0)))
            put(out, rows, parts[1], f1)
            f2 = minus(get(block, rows, parts[2]), complex_dot(f0, tile(1)))
            put(out, rows, parts[2], minus(f2, complex_dot(cuts(f1), tile(2))))
            return carry

        lax.fori_loop(0, TS, chunk, 0)
        long = SIDE // HALVES
        for half in range(HALVES):
            rows = slice(half * long, (half + 1) * long)
            wide = [x for cols in parts[1:] for x in get(out, rows, cols)]
            store_piece(along_row[half], jnp.concatenate(wide, 1))

    @pl.when((role[0] == 0) & (role[1] > 0))
    def _():
        def tile(t):
            return [(row_high[parts[t], cols], row_low[parts[t], cols]) for cols in parts[:2]]

        def chunk(j, carry):
            cols = pl.ds(pl.multiple_of(j * TILE, TILE), TILE)
            p0 = get(block, parts[0], cols)
            put(out, parts[0], cols, p0)
            p0 = cuts(p0)
            p1 = minus(get(block, parts[1], cols), complex_dot(tile(0), p0))
            put(out, parts[1], cols, p1)
            p2 = minus(get(block, parts[2], cols), complex_dot(tile(1), p0))
            put(out, parts[2], cols, minus(p2, complex_dot(tile(2), cuts(p1))))
            return carry

        lax.fori_loop(0, TS, chunk, 0)
        for half in range(HALVES):
            both = get(out, parts[half + 1], slice(0, SIDE))
            store_piece(along_col[half], jnp.concatenate(both, 0))

    @pl.when((role[0] > 0) & (role[1] > 0))
    def _():
        def chunk(i, carry):
            rows = pl.ds(pl.multiple_of(i * TILE, TILE), TILE)
            trailing(block, out, rows, (row_high, row_low), (col_high, col_low))
            return carry

        lax.fori_loop(0, TS, chunk, 0)


def panel(role, block, from_row, from_col):
    return pl.pallas_call(
        panel_kernel,
        in_specs=[SCALAR] + [HELD] * (1 + 2 * ARRIVALS),
        out_specs=[HELD] * (1 + 2 * HALVES),
        out_shape=[jax.ShapeDtypeStruct(block.shape, F32)] + pieces_of(2),
        scratch_shapes=piece_scratch(1),
        compiler_params=pltpu.CompilerParams(vmem_limit_bytes=VMEM_BYTES),
    )(role, block, *from_row, *from_col)


def trail_kernel(role, block, *refs):
    from_row, from_col = refs[:ARRIVALS], refs[ARRIVALS : 2 * ARRIVALS]
    out, held, row_high, row_low, col_high, col_low, sem, sems = refs[2 * ARRIVALS :]
    inner = (role[0] > 0) & (role[1] > 0)

    @pl.when(jnp.logical_not(inner))
    def _():
        store = pltpu.make_async_copy(block, out, sem)
        store.start()
        store.wait()

    @pl.when(inner)
    def _():
        unpack(from_row, role[1], row_high, row_low)
        unpack(from_col, role[0], col_high, col_low)

        def store(i):
            rows = pl.ds(pl.multiple_of(i * TILE, TILE), TILE)
            return pltpu.make_async_copy(held.at[:, rows, :], out.at[:, rows, :], sems.at[i])

        def chunk(i, carry):
            rows = pl.ds(pl.multiple_of(i * TILE, TILE), TILE)
            trailing(block, held, rows, (row_high, row_low), (col_high, col_low))
            store(i).start()
            return carry

        lax.fori_loop(0, TS, chunk, 0)
        for i in range(TS):
            store(i).wait()


def trail(role, block, from_row, from_col):
    return pl.pallas_call(
        trail_kernel,
        in_specs=[SCALAR] + [HELD] * (1 + 2 * ARRIVALS),
        out_specs=IN_HBM,
        out_shape=jax.ShapeDtypeStruct(block.shape, F32),
        scratch_shapes=[pltpu.VMEM(block.shape, F32)]
        + piece_scratch(2)
        + [pltpu.SemaphoreType.DMA, pltpu.SemaphoreType.DMA((TS,))],
        compiler_params=pltpu.CompilerParams(vmem_limit_bytes=VMEM_BYTES),
    )(role, block, *from_row, *from_col)


def broadcast(halves, axis):
    first = lax.axis_index(axis) == 0
    one = lax.ppermute(halves[0], axis, [(0, 1)])
    three = lax.ppermute(halves[1], axis, [(0, 3)])
    plus = lax.ppermute(jnp.where(first, halves[1], one), axis, [(0, 1), (1, 2)])
    minus = lax.ppermute(jnp.where(first, halves[0], three), axis, [(0, 3), (3, 2)])
    return one, three, plus, minus


def body(
    parent_front,
    child_left,
    child_right,
    tile_ranks,
    destination,
    tile_place,
    row_source,
    col_source,
    own_left,
    own_right,
    own_place,
    pivot_inverse,
):
    joined = ("front", "row")
    role = jnp.stack([lax.axis_index("row"), lax.axis_index("col")]).astype(jnp.int32)

    def sent(second):
        slots = pack(
            second,
            destination,
            tile_place,
            tile_ranks,
            child_left,
            child_right,
            row_source,
            col_source,
        )
        return lax.all_to_all(slots, joined, split_axis=0, concat_axis=0, tiled=True)

    second_slots = sent(1)
    first_slots = sent(0)
    places = second_slots[:, TILE + 2 * RANK : TILE + 2 * RANK + 2, 0].astype(jnp.int32)

    block = add_first(places[:, 0], own_place, parent_front[0], own_left, own_right, second_slots)
    block, *pieces = add_second(places[:, 1], role, block, first_slots, pivot_inverse[0])
    from_row, from_col = broadcast(pieces[:HALVES], "col"), broadcast(pieces[HALVES:], "row")
    block, *pieces = panel(role, block, from_row, from_col)
    from_row, from_col = broadcast(pieces[:HALVES], "col"), broadcast(pieces[HALVES:], "row")
    return trail(role, block, from_row, from_col)[None]


def solution(mesh):
    joined = ("front", "row", "col")
    tiles = P(joined, None, None)
    return jax.shard_map(
        body,
        mesh=mesh,
        in_specs=(
            P("front", None, "row", "col"),
            tiles,
            tiles,
            P(joined),
            P(joined),
            P(joined),
            P(joined, None),
            P(joined, None),
            tiles,
            tiles,
            P(joined),
            P("front", None, None, None, None),
        ),
        out_specs=P("front", None, "row", "col"),
        check_vma=False,
    )
```

```python
import functools
import math

import jax
import jax.numpy as jnp
from jax import lax
from jax.experimental import pallas as pl
from jax.experimental.pallas import tpu as pltpu
from jax.sharding import PartitionSpec as P

TILE = 256
RANK = 128
TS = 3
SIDE = TS * TILE
SENT = 28
GROUP = 32
HALVES = 2
ARRIVALS = 4
CHUNK = 64
LONG = SIDE // HALVES
CODE_ROWS = 16
NOTE_ROWS = 16
LOG_STEP = math.log(2.0) / 32.0
VMEM_BYTES = 32 * 1024 * 1024
MORE_VMEM_BYTES = 45 * 1024 * 1024
ALL_VMEM_BYTES = 60 * 1024 * 1024
DEPTH = 4
BF16 = jnp.bfloat16
F32 = jnp.float32
IN_HBM = pl.BlockSpec(memory_space=pltpu.HBM)
HELD = pl.BlockSpec(memory_space=pltpu.VMEM)
SCALAR = pl.BlockSpec(memory_space=pltpu.SMEM)


def encode(values):
    peak = jnp.maximum(jnp.max(jnp.abs(values), axis=0, keepdims=True), 1e-30)
    code = jnp.ceil(jnp.log(peak * (1.0 / 32700.0)) * (1.0 / LOG_STEP))
    whole = jnp.round(values * jnp.exp(code * -LOG_STEP))
    whole = jnp.clip(whole, -32767.0, 32767.0).astype(jnp.int32)
    code_rows = jnp.broadcast_to(code.astype(jnp.int32), (CODE_ROWS, values.shape[1]))
    return whole.astype(jnp.int16), code_rows.astype(jnp.int16)


def store_piece(ref, values):
    rows = values.shape[0]
    whole, code_rows = encode(values)
    ref[:rows, :] = whole
    ref[rows:, :] = code_rows


def cut(x):
    high = x.astype(BF16)
    return high, (x - high.astype(F32)).astype(BF16)


def dot(a, b):
    return lax.dot_general(a, b, (((1,), (0,)), ((), ())), preferred_element_type=F32)


def dot_cut(a, b):
    return dot(a[0], b[0]) + (dot(a[0], b[1]) + dot(a[1], b[0]))


def cuts(pair):
    return [cut(x) for x in pair]


def complex_dot(a, b):
    return (
        dot_cut(a[0], b[0]) - dot_cut(a[1], b[1]),
        dot_cut(a[0], b[1]) + dot_cut(a[1], b[0]),
    )


def minus(a, b):
    return a[0] - b[0], a[1] - b[1]


def pack_kernel(
    second, destination, place, ranks, left, right, rows, cols, out, *scratch
):
    number, order, lefts, rights, packed, notes, sem_in, sem_out, sem_notes = scratch

    def clear(d, carry):
        number[0, d] = -1
        number[1, d] = -1
        return carry

    lax.fori_loop(0, GROUP, clear, 0)

    def sort(k, count):
        d = destination[k]
        later = (number[0, d] >= 0).astype(jnp.int32)
        number[later, d] = k
        mine = later == second

        @pl.when(mine)
        def _():
            order[count] = k

        return count + mine.astype(jnp.int32)

    count = lax.fori_loop(0, SENT, sort, 0)

    def fetch(p, slot):
        k = order[p]
        return (
            pltpu.make_async_copy(left.at[k], lefts.at[slot], sem_in.at[slot, 0]),
            pltpu.make_async_copy(right.at[k], rights.at[slot], sem_in.at[slot, 1]),
        )

    def store(d, slot):
        target = out.at[d, pl.ds(0, TILE + 2 * RANK)]
        return pltpu.make_async_copy(packed.at[slot], target, sem_out.at[slot])

    for slot in range(DEPTH):

        @pl.when(slot < count)
        def _(slot=slot):
            for copy in fetch(slot, slot):
                copy.start()

    if second:
        line = lax.broadcasted_iota(jnp.int32, (NOTE_ROWS, TILE), 0)

        def note(d, carry):
            def code(which):
                k = number[which, d]
                return jnp.where(k >= 0, place[jnp.maximum(k, 0)], -1)

            lines = jnp.where(line == 0, code(1), code(0))
            notes[d] = lines.astype(F32).astype(BF16)
            return carry

        lax.fori_loop(0, GROUP, note, 0)
        tell = pltpu.make_async_copy(
            notes, out.at[:, pl.ds(TILE + 2 * RANK, NOTE_ROWS)], sem_notes
        )
        tell.start()

    index = lax.broadcasted_iota(jnp.int32, (TILE, TILE), 0)
    width = lax.broadcasted_iota(jnp.int32, (TILE, 2 * RANK), 1)
    width = jnp.where(width >= RANK, width - RANK, width)
    turned = (((0,), (0,)), ((), ()))

    def onehot(chosen):
        return jnp.where(index == chosen, 1.0, 0.0).astype(BF16)

    def work(p, carry):
        slot = p & (DEPTH - 1)
        k = order[p]
        for copy in fetch(p, slot):
            copy.wait()

        @pl.when(p >= DEPTH)
        def _():
            store(0, slot).wait()

        moved = lax.dot_general(
            onehot(rows[pl.ds(k, 1), :]), lefts[slot], turned, preferred_element_type=F32
        )
        packed[slot, :TILE, :] = jnp.where(width < ranks[k], moved, 0.0).astype(BF16)
        packed[slot, TILE:, :] = lax.dot_general(
            rights[slot], onehot(cols[pl.ds(k, 1), :]), turned, preferred_element_type=F32
        ).astype(BF16)
        store(destination[k], slot).start()

        @pl.when(p + DEPTH < count)
        def _():
            for copy in fetch(p + DEPTH, slot):
                copy.start()

        return carry

    lax.fori_loop(0, count, work, 0)
    for slot in range(DEPTH):

        @pl.when(slot < count)
        def _(slot=slot):
            store(0, slot).wait()

    if second:
        tell.wait()


def pack(second, destination, place, ranks, left, right, rows, cols):
    depth = TILE + 2 * RANK + (NOTE_ROWS if second else 0)
    tiles = pltpu.VMEM((DEPTH, TILE, 2 * RANK), BF16)
    return pl.pallas_call(
        functools.partial(pack_kernel, second),
        in_specs=[SCALAR] * 3 + [IN_HBM] * 2 + [HELD] * 2,
        out_specs=IN_HBM,
        out_shape=jax.ShapeDtypeStruct((GROUP, depth, TILE), BF16),
        scratch_shapes=[
            pltpu.SMEM((2, GROUP), jnp.int32),
            pltpu.SMEM((SENT,), jnp.int32),
            tiles,
            tiles,
            pltpu.VMEM((DEPTH, TILE + 2 * RANK, TILE), BF16),
            pltpu.VMEM((GROUP, NOTE_ROWS, TILE), BF16),
            pltpu.SemaphoreType.DMA((DEPTH, 2)),
            pltpu.SemaphoreType.DMA((DEPTH,)),
            pltpu.SemaphoreType.DMA,
        ],
        compiler_params=pltpu.CompilerParams(vmem_limit_bytes=ALL_VMEM_BYTES),
        cost_estimate=pl.CostEstimate(
            flops=4 * SENT * TILE**3, bytes_accessed=16 * 2**20, transcendentals=0
        ),
    )(destination, place, ranks, left, right, rows, cols)


def add_at(out, place, real, imag):
    a = place // TS
    rows = pl.ds(pl.multiple_of(a * TILE, TILE), TILE)
    cols = pl.ds(pl.multiple_of((place - a * TS) * TILE, TILE), TILE)
    out[0, rows, cols] += real
    out[1, rows, cols] += imag


def add_own(out, place, left, right):
    real_side = jnp.concatenate([right[:, :RANK], -right[:, RANK:]], 1)
    imag_side = jnp.concatenate([right[:, RANK:], right[:, :RANK]], 1)
    contract = (((1,), (1,)), ((), ()))
    add_at(
        out,
        place,
        lax.dot_general(left, real_side, contract, preferred_element_type=F32),
        lax.dot_general(left, imag_side, contract, preferred_element_type=F32),
    )


def add_slots(out, places, slots, scratch, prepare):
    order, arrived, sems = scratch

    def sort(slot, count):
        mine = places[slot] >= 0

        @pl.when(mine)
        def _():
            order[count] = slot

        return count + mine.astype(jnp.int32)

    count = lax.fori_loop(0, GROUP, sort, 0)

    def fetch(p, held):
        source = slots.at[order[p], pl.ds(0, TILE + 2 * RANK)]
        return pltpu.make_async_copy(source, arrived.at[held], sems.at[held])

    for p in range(DEPTH):

        @pl.when(p < count)
        def _(p=p):
            fetch(p, p).start()

    prepare()

    def work(p, carry):
        held = p & (DEPTH - 1)
        fetch(p, held).wait()
        left = arrived[held, :TILE, :]
        top = arrived[held, TILE : TILE + RANK, :]
        bottom = arrived[held, TILE + RANK :, :]
        add_at(
            out,
            places[order[p]],
            dot(left, jnp.concatenate([top, -bottom], 0)),
            dot(left, jnp.concatenate([bottom, top], 0)),
        )

        @pl.when(p + DEPTH < count)
        def _():
            fetch(p + DEPTH, held).start()

        return carry

    lax.fori_loop(0, count, work, 0)


def add_scratch():
    return [
        pltpu.SMEM((GROUP,), jnp.int32),
        pltpu.VMEM((DEPTH, TILE + 2 * RANK, TILE), BF16),
        pltpu.SemaphoreType.DMA((DEPTH,)),
    ]


def first_kernel(places, own_places, before, own_left, own_right, slots, out, *scratch):
    def prepare():
        pltpu.sync_copy(before, out)

        def own_step(j, carry):
            add_own(out, own_places[j], own_left[j], own_right[j])
            return carry

        lax.fori_loop(0, own_left.shape[0], own_step, 0)

    add_slots(out, places, slots, scratch, prepare)


def tile_at(i, j):
    return slice(i * TILE, (i + 1) * TILE), slice(j * TILE, (j + 1) * TILE)


def get(ref, rows, cols):
    return ref[0, rows, cols], ref[1, rows, cols]


def put(ref, rows, cols, value):
    ref[0, rows, cols] = value[0]
    ref[1, rows, cols] = value[1]


def second_kernel(places, role, before, slots, inverse, out, *refs):
    along_row, along_col = refs[:HALVES], refs[HALVES : 2 * HALVES]

    def prepare():
        out[...] = before[...]

    add_slots(out, places, slots, refs[2 * HALVES :], prepare)

    @pl.when((role[0] == 0) & (role[1] == 0))
    def _():
        pivots = [cuts((inverse[p, 0], inverse[p, 1])) for p in range(TS)]
        for p in range(TS - 1):
            uppers = {j: cuts(get(out, *tile_at(p, j))) for j in range(p + 1, TS)}
            for i in range(p + 1, TS):
                factor = complex_dot(cuts(get(out, *tile_at(i, p))), pivots[p])
                put(out, *tile_at(i, p), factor)
                factor = cuts(factor)
                for j in range(p + 1, TS):
                    at = tile_at(i, j)
                    put(out, *at, minus(get(out, *at), complex_dot(factor, uppers[j])))
        lower = [get(out, *tile_at(i, j)) for i, j in ((1, 0), (2, 0), (2, 1))]
        lower = jnp.concatenate([jnp.concatenate(x, 1) for x in lower], 0)
        upper = [
            complex_dot(cuts(get(out, *tile_at(i, j))), pivots[j])
            for i, j in ((0, 1), (0, 2), (1, 2))
        ]
        upper = [jnp.concatenate([x[half] for x in upper], 1) for half in (0, 1)]
        for half in range(HALVES):
            store_piece(along_row[half], lower[half * LONG : (half + 1) * LONG])
            store_piece(along_col[half], upper[half])

    @pl.when((role[0] > 0) & (role[1] == 0))
    def _():
        for p in range(TS):
            pivot = cuts((inverse[p, 0], inverse[p, 1]))
            for i in range(TS):
                at = tile_at(i, p)
                put(out, *at, complex_dot(cuts(get(out, *at)), pivot))
        for half in range(HALVES):
            rows = slice(half * LONG, (half + 1) * LONG)
            store_piece(along_row[half], jnp.concatenate(get(out, rows, slice(0, TILE)), 1))

    @pl.when((role[0] == 0) & (role[1] > 0))
    def _():
        for half in range(HALVES):
            store_piece(along_col[half], out[half, :TILE, :])


ADD_COST = pl.CostEstimate(
    flops=4 * GROUP * TILE**3, bytes_accessed=20 * 2**20, transcendentals=0
)


def add_first(places, own_places, before, own_left, own_right, slots):
    return pl.pallas_call(
        first_kernel,
        in_specs=[SCALAR, SCALAR, IN_HBM, HELD, HELD, IN_HBM],
        out_specs=HELD,
        out_shape=jax.ShapeDtypeStruct(before.shape, F32),
        scratch_shapes=add_scratch(),
        compiler_params=pltpu.CompilerParams(vmem_limit_bytes=MORE_VMEM_BYTES),
        cost_estimate=ADD_COST,
    )(places, own_places, before, own_left, own_right, slots)


def row_shape(panels):
    return (SIDE // HALVES + CODE_ROWS, 2 * TILE * panels)


def col_shape(panels):
    return (2 * TILE * panels // HALVES + CODE_ROWS, SIDE)


def coded(shape):
    return jax.ShapeDtypeStruct(shape, jnp.int16)


def pieces_of(panels):
    return [coded(row_shape(panels))] * HALVES + [coded(col_shape(panels))] * HALVES


def add_second(places, role, before, slots, inverse):
    return pl.pallas_call(
        second_kernel,
        in_specs=[SCALAR, SCALAR, HELD, IN_HBM, HELD],
        out_specs=[HELD] * (1 + 2 * HALVES),
        out_shape=[jax.ShapeDtypeStruct(before.shape, F32)] + pieces_of(1),
        scratch_shapes=add_scratch(),
        compiler_params=pltpu.CompilerParams(vmem_limit_bytes=MORE_VMEM_BYTES),
        cost_estimate=ADD_COST,
    )(places, role, before, slots, inverse)


def scales(code_rows):
    return jnp.exp(code_rows[:1].astype(jnp.int32).astype(F32) * LOG_STEP)


def unpack(refs, place, high, low):
    one, three, plus, minus = refs
    half = one.shape[0] - CODE_ROWS
    for at, pair in ((1, (one, plus)), (2, (plus, minus)), (3, (minus, three))):

        @pl.when(place == at)
        def _(pair=pair):
            for which, ref in enumerate(pair):
                scale = scales(ref[half:, :])

                def chunk(i, carry, ref=ref, scale=scale, which=which):
                    rows = pl.ds(pl.multiple_of(i * CHUNK, CHUNK), CHUNK)
                    into = pl.ds(pl.multiple_of(which * half + i * CHUNK, CHUNK), CHUNK)
                    values = ref[rows, :].astype(jnp.int32).astype(F32) * scale
                    high[into, :], low[into, :] = cut(values)
                    return carry

                lax.fori_loop(0, half // CHUNK, chunk, 0)


def trailing(block, out, rows, left, right):
    panels = left[0].shape[1] // (2 * TILE)

    def turned(x, imag):
        parts = []
        for p in range(panels):
            a = x[rows, 2 * p * TILE : (2 * p + 1) * TILE]
            b = x[rows, (2 * p + 1) * TILE : (2 * p + 2) * TILE]
            parts += [b, a] if imag else [a, -b]
        return jnp.concatenate(parts, 1)

    for half in (0, 1):
        a = [turned(x, half == 1) for x in left]
        for j in range(TS):
            cols = slice(j * TILE, (j + 1) * TILE)
            product = dot_cut(a, [x[:, cols] for x in right])
            out[half, rows, cols] = block[half, rows, cols] - product


def piece_scratch(panels):
    return [pltpu.VMEM((SIDE, 2 * TILE * panels), BF16)] * 2 + [
        pltpu.VMEM((2 * TILE * panels, SIDE), BF16)
    ] * 2


def panel_kernel(role, block, *refs):
    from_row, from_col = refs[:ARRIVALS], refs[ARRIVALS : 2 * ARRIVALS]
    out, *halves = refs[2 * ARRIVALS : 2 * ARRIVALS + 1 + HALVES]
    row_high, row_low, col_high, col_low = refs[2 * ARRIVALS + 1 + HALVES :]
    parts = [slice(t * TILE, (t + 1) * TILE) for t in range(TS)]

    @pl.when(role[1] > 0)
    def _():
        unpack(from_row, role[1], row_high, row_low)

    @pl.when(role[0] > 0)
    def _():
        unpack(from_col, role[0], col_high, col_low)

    @pl.when((role[0] == 0) & (role[1] == 0))
    def _():
        out[...] = block[...]

    @pl.when((role[0] > 0) & (role[1] == 0))
    def _():
        def tile(t):
            return [(col_high[rows, parts[t]], col_low[rows, parts[t]]) for rows in parts[:2]]

        def chunk(i, carry):
            rows = pl.ds(pl.multiple_of(i * TILE, TILE), TILE)
            f0 = get(block, rows, parts[0])
            put(out, rows, parts[0], f0)
            f0 = cuts(f0)
            f1 = minus(get(block, rows, parts[1]), complex_dot(f0, tile(0)))
            put(out, rows, parts[1], f1)
            f2 = minus(get(block, rows, parts[2]), complex_dot(f0, tile(1)))
            put(out, rows, parts[2], minus(f2, complex_dot(cuts(f1), tile(2))))
            return carry

        lax.fori_loop(0, TS, chunk, 0)
        for which, ref in enumerate(halves):
            half = which ^ (role[0] == ROW_TURNED).astype(jnp.int32)
            rows = pl.ds(pl.multiple_of(half * LONG, LONG), LONG)
            wide = [x for cols in parts[1:] for x in get(out, rows, cols)]
            store_piece(ref, jnp.concatenate(wide, 1))

    @pl.when((role[0] == 0) & (role[1] > 0))
    def _():
        def tile(t):
            return [(row_high[parts[t], cols], row_low[parts[t], cols]) for cols in parts[:2]]

        def chunk(j, carry):
            cols = pl.ds(pl.multiple_of(j * TILE, TILE), TILE)
            p0 = get(block, parts[0], cols)
            put(out, parts[0], cols, p0)
            p0 = cuts(p0)
            p1 = minus(get(block, parts[1], cols), complex_dot(tile(0), p0))
            put(out, parts[1], cols, p1)
            p2 = minus(get(block, parts[2], cols), complex_dot(tile(1), p0))
            put(out, parts[2], cols, minus(p2, complex_dot(tile(2), cuts(p1))))
            return carry

        lax.fori_loop(0, TS, chunk, 0)
        for which, ref in enumerate(halves):
            half = which ^ (role[1] == COL_TURNED).astype(jnp.int32)
            rows = pl.ds(pl.multiple_of((half + 1) * TILE, TILE), TILE)
            tall = jnp.concatenate(get(out, rows, slice(0, SIDE)), 0)
            rest = jnp.concatenate([tall[LONG:, cols] for cols in parts], 0)
            store_piece(ref, jnp.concatenate([tall[:LONG], rest], 1))

    @pl.when((role[0] > 0) & (role[1] > 0))
    def _():
        def chunk(i, carry):
            rows = pl.ds(pl.multiple_of(i * TILE, TILE), TILE)
            trailing(block, out, rows, (row_high, row_low), (col_high, col_low))
            return carry

        lax.fori_loop(0, TS, chunk, 0)


def panel(role, block, from_row, from_col):
    return pl.pallas_call(
        panel_kernel,
        in_specs=[SCALAR] + [HELD] * (1 + 2 * ARRIVALS),
        out_specs=[HELD] * (1 + HALVES),
        out_shape=[jax.ShapeDtypeStruct(block.shape, F32)] + [coded(row_shape(2))] * HALVES,
        scratch_shapes=piece_scratch(1),
        compiler_params=pltpu.CompilerParams(vmem_limit_bytes=VMEM_BYTES),
    )(role, block, *from_row, *from_col)


def trail_kernel(role, source, block, *refs):
    moved = refs[:MOVES]
    out, held, got, row_high, row_low, col_high, col_low, sem, sems, got_sems = refs[MOVES:]
    inner = (role[0] > 0) & (role[1] > 0)

    @pl.when(jnp.logical_not(inner))
    def _():
        store = pltpu.make_async_copy(block, out, sem)
        store.start()
        store.wait()

    @pl.when(inner)
    def _():
        first = (role[0] * 4 + role[1]) * 2 * HALVES
        for k in range(2 * HALVES):
            for m in range(MOVES):

                @pl.when(source[first + k] == m)
                def _(k=k, m=m):
                    pltpu.make_async_copy(moved[m], got.at[k], got_sems.at[k]).start()

        for k in range(2 * HALVES):
            pltpu.make_async_copy(moved[0], got.at[k], got_sems.at[k]).wait()
            scale = scales(got[k, LONG:, :])
            half = k % HALVES

            def chunk(i, carry, k=k, half=half, scale=scale):
                rows = pl.ds(pl.multiple_of(i * CHUNK, CHUNK), CHUNK)
                high, low = cut(got[k, rows, :].astype(jnp.int32).astype(F32) * scale)
                if k < HALVES:
                    into = pl.ds(pl.multiple_of(half * LONG + i * CHUNK, CHUNK), CHUNK)
                    row_high[into, :], row_low[into, :] = high, low
                else:
                    start = half * 2 * TILE + i * CHUNK
                    into = pl.ds(pl.multiple_of(start, CHUNK), CHUNK)
                    col_high[into, :], col_low[into, :] = high[:, :SIDE], low[:, :SIDE]
                    start = half * 2 * TILE + LONG + (i & 1) * CHUNK
                    into = pl.ds(pl.multiple_of(start, CHUNK), CHUNK)
                    cols = pl.ds(pl.multiple_of((i >> 1) * TILE, TILE), TILE)
                    col_high[into, cols], col_low[into, cols] = high[:, SIDE:], low[:, SIDE:]
                return carry

            lax.fori_loop(0, LONG // CHUNK, chunk, 0)

        def store(i):
            rows = pl.ds(pl.multiple_of(i * TILE, TILE), TILE)
            return pltpu.make_async_copy(held.at[:, rows, :], out.at[:, rows, :], sems.at[i])

        def chunk(i, carry):
            rows = pl.ds(pl.multiple_of(i * TILE, TILE), TILE)
            trailing(block, held, rows, (row_high, row_low), (col_high, col_low))
            store(i).start()
            return carry

        lax.fori_loop(0, TS, chunk, 0)
        for i in range(TS):
            store(i).wait()


def trail(role, source, block, moved):
    return pl.pallas_call(
        trail_kernel,
        in_specs=[SCALAR] * 2 + [HELD] * (1 + MOVES),
        out_specs=IN_HBM,
        out_shape=jax.ShapeDtypeStruct(block.shape, F32),
        scratch_shapes=[
            pltpu.VMEM(block.shape, F32),
            pltpu.VMEM((2 * HALVES,) + row_shape(2), jnp.int16),
        ]
        + piece_scratch(2)
        + [
            pltpu.SemaphoreType.DMA,
            pltpu.SemaphoreType.DMA((TS,)),
            pltpu.SemaphoreType.DMA((2 * HALVES,)),
        ],
        compiler_params=pltpu.CompilerParams(vmem_limit_bytes=VMEM_BYTES),
    )(role, source, block, *moved)


ROW_WAY = {1: 1, 2: 1, 3: 3}
COL_WAY = {1: 3, 2: 1, 3: 1}
ROW_TURNED, COL_TURNED = 3, 1
MOVES = 8


def ways(turn):
    def way(table, line):
        return 4 - table[line] if turn else table[line]

    return [(r, way(ROW_WAY, r)) for r in ROW_WAY], [(way(COL_WAY, c), c) for c in COL_WAY]


def move_all(halves):
    def move(array, pairs):
        pairs = [(4 * a + b, 4 * c + d) for (a, b), (c, d) in pairs]
        return lax.ppermute(array, ("row", "col"), pairs)

    out, on, late = [], [], []
    for turn in (0, 1):
        rows, cols = ways(turn)
        out.append([((r, 0), (r, c)) for r, c in rows] + [((0, c), (r, c)) for r, c in cols])
        on.append(
            [((r, c), (r, 2)) for r, c in rows] + [((r, c), (2, c)) for r, c in cols if c != 2]
        )
        late.append([((r, c), (2, c)) for r, c in cols if c == 2])
    first = [move(halves[turn], out[turn]) for turn in (0, 1)]
    second = [move(halves[1 - turn], out[turn]) for turn in (0, 1)]
    onward = [move(first[turn], on[turn]) for turn in (0, 1)]
    return first + second + onward + [move(first[turn], late[turn]) for turn in (0, 1)]


def sources():
    table = [0] * (16 * 2 * HALVES)

    def enter(row, col, slot, half, array):
        table[(row * 4 + col) * 2 * HALVES + slot * HALVES + half] = array

    for turn in (0, 1):
        rows, cols = ways(turn)
        for slot, devices in ((0, rows), (1, cols)):
            for r, c in devices:
                half = 0 if (c if slot == 0 else r) == 1 else 1
                enter(r, c, slot, half, turn)
                enter(r, c, slot, 1 - half, 2 + turn)
                middle = (r, 2) if slot == 0 else (2, c)
                both = slot == 1 and c == 2
                enter(*middle, slot, half, (6 if both else 4) + turn)
    return table


def broadcast(halves, axis):
    first = lax.axis_index(axis) == 0
    one = lax.ppermute(halves[0], axis, [(0, 1)])
    three = lax.ppermute(halves[1], axis, [(0, 3)])
    plus = lax.ppermute(jnp.where(first, halves[1], one), axis, [(0, 1), (1, 2)])
    minus = lax.ppermute(jnp.where(first, halves[0], three), axis, [(0, 3), (3, 2)])
    return one, three, plus, minus


def body(
    parent_front,
    child_left,
    child_right,
    tile_ranks,
    destination,
    tile_place,
    row_source,
    col_source,
    own_left,
    own_right,
    own_place,
    pivot_inverse,
):
    joined = ("front", "row")
    role = jnp.stack([lax.axis_index("row"), lax.axis_index("col")]).astype(jnp.int32)

    def sent(second):
        slots = pack(
            second,
            destination,
            tile_place,
            tile_ranks,
            child_left,
            child_right,
            row_source,
            col_source,
        )
        return lax.all_to_all(slots, joined, split_axis=0, concat_axis=0, tiled=True)

    second_slots = sent(1)
    first_slots = sent(0)
    places = second_slots[:, TILE + 2 * RANK : TILE + 2 * RANK + 2, 0].astype(jnp.int32)

    block = add_first(places[:, 0], own_place, parent_front[0], own_left, own_right, second_slots)
    block, *pieces = add_second(places[:, 1], role, block, first_slots, pivot_inverse[0])
    from_row, from_col = broadcast(pieces[:HALVES], "col"), broadcast(pieces[HALVES:], "row")
    block, *halves = panel(role, block, from_row, from_col)
    return trail(role, jnp.array(sources(), jnp.int32), block, move_all(halves))[None]


def solution(mesh):
    joined = ("front", "row", "col")
    tiles = P(joined, None, None)
    return jax.shard_map(
        body,
        mesh=mesh,
        in_specs=(
            P("front", None, "row", "col"),
            tiles,
            tiles,
            P(joined),
            P(joined),
            P(joined),
            P(joined, None),
            P(joined, None),
            tiles,
            tiles,
            P(joined),
            P("front", None, None, None, None),
        ),
        out_specs=P("front", None, "row", "col"),
        check_vma=False,
    )
```

```python
import functools
import math

import jax
import jax.numpy as jnp
from jax import lax
from jax.experimental import pallas as pl
from jax.experimental.pallas import tpu as pltpu
from jax.sharding import PartitionSpec as P

TILE = 256
RANK = 128
TS = 3
SIDE = TS * TILE
SENT = 28
GROUP = 32
HALVES = 2
ARRIVALS = 4
CHUNK = 64
LONG = SIDE // HALVES
CODE_ROWS = 16
NOTE_ROWS = 16
LOG_STEP = math.log(2.0) / 32.0
VMEM_BYTES = 32 * 1024 * 1024
MORE_VMEM_BYTES = 45 * 1024 * 1024
ALL_VMEM_BYTES = 60 * 1024 * 1024
DEPTH = 4
BF16 = jnp.bfloat16
F32 = jnp.float32
IN_HBM = pl.BlockSpec(memory_space=pltpu.HBM)
HELD = pl.BlockSpec(memory_space=pltpu.VMEM)
SCALAR = pl.BlockSpec(memory_space=pltpu.SMEM)


def encode(values):
    peak = jnp.maximum(jnp.max(jnp.abs(values), axis=0, keepdims=True), 1e-30)
    code = jnp.ceil(jnp.log(peak * (1.0 / 32700.0)) * (1.0 / LOG_STEP))
    whole = jnp.round(values * jnp.exp(code * -LOG_STEP))
    whole = jnp.clip(whole, -32767.0, 32767.0).astype(jnp.int32)
    code_rows = jnp.broadcast_to(code.astype(jnp.int32), (CODE_ROWS, values.shape[1]))
    return whole.astype(jnp.int16), code_rows.astype(jnp.int16)


def store_piece(ref, values):
    rows = values.shape[0]
    whole, code_rows = encode(values)
    ref[:rows, :] = whole
    ref[rows:, :] = code_rows


def cut(x):
    high = x.astype(BF16)
    return high, (x - high.astype(F32)).astype(BF16)


def dot(a, b):
    return lax.dot_general(a, b, (((1,), (0,)), ((), ())), preferred_element_type=F32)


def dot_cut(a, b):
    return dot(a[0], b[0]) + (dot(a[0], b[1]) + dot(a[1], b[0]))


def cuts(pair):
    return [cut(x) for x in pair]


def complex_dot(a, b):
    return (
        dot_cut(a[0], b[0]) - dot_cut(a[1], b[1]),
        dot_cut(a[0], b[1]) + dot_cut(a[1], b[0]),
    )


def minus(a, b):
    return a[0] - b[0], a[1] - b[1]


def pack_kernel(
    second, destination, place, ranks, left, right, rows, cols, out, *scratch
):
    number, order, lefts, rights, packed, notes, sem_in, sem_out, sem_notes = scratch

    def clear(d, carry):
        number[0, d] = -1
        number[1, d] = -1
        return carry

    lax.fori_loop(0, GROUP, clear, 0)

    def sort(k, count):
        d = destination[k]
        later = (number[0, d] >= 0).astype(jnp.int32)
        number[later, d] = k
        mine = later == second

        @pl.when(mine)
        def _():
            order[count] = k

        return count + mine.astype(jnp.int32)

    count = lax.fori_loop(0, SENT, sort, 0)

    def fetch(p, slot):
        k = order[p]
        return (
            pltpu.make_async_copy(left.at[k], lefts.at[slot], sem_in.at[slot, 0]),
            pltpu.make_async_copy(right.at[k], rights.at[slot], sem_in.at[slot, 1]),
        )

    def store(d, slot):
        target = out.at[d, pl.ds(0, TILE + 2 * RANK)]
        return pltpu.make_async_copy(packed.at[slot], target, sem_out.at[slot])

    for slot in range(DEPTH):

        @pl.when(slot < count)
        def _(slot=slot):
            for copy in fetch(slot, slot):
                copy.start()

    if second:
        line = lax.broadcasted_iota(jnp.int32, (NOTE_ROWS, TILE), 0)

        def note(d, carry):
            def code(which):
                k = number[which, d]
                return jnp.where(k >= 0, place[jnp.maximum(k, 0)], -1)

            lines = jnp.where(line == 0, code(1), code(0))
            notes[d] = lines.astype(F32).astype(BF16)
            return carry

        lax.fori_loop(0, GROUP, note, 0)
        tell = pltpu.make_async_copy(
            notes, out.at[:, pl.ds(TILE + 2 * RANK, NOTE_ROWS)], sem_notes
        )
        tell.start()

    index = lax.broadcasted_iota(jnp.int32, (TILE, TILE), 0)
    width = lax.broadcasted_iota(jnp.int32, (TILE, 2 * RANK), 1)
    width = jnp.where(width >= RANK, width - RANK, width)
    turned = (((0,), (0,)), ((), ()))

    def onehot(chosen):
        return jnp.where(index == chosen, 1.0, 0.0).astype(BF16)

    def work(p, carry):
        slot = p & (DEPTH - 1)
        k = order[p]
        for copy in fetch(p, slot):
            copy.wait()

        @pl.when(p >= DEPTH)
        def _():
            store(0, slot).wait()

        moved = lax.dot_general(
            onehot(rows[pl.ds(k, 1), :]), lefts[slot], turned, preferred_element_type=F32
        )
        packed[slot, :TILE, :] = jnp.where(width < ranks[k], moved, 0.0).astype(BF16)
        packed[slot, TILE:, :] = lax.dot_general(
            rights[slot], onehot(cols[pl.ds(k, 1), :]), turned, preferred_element_type=F32
        ).astype(BF16)
        store(destination[k], slot).start()

        @pl.when(p + DEPTH < count)
        def _():
            for copy in fetch(p + DEPTH, slot):
                copy.start()

        return carry

    lax.fori_loop(0, count, work, 0)
    for slot in range(DEPTH):

        @pl.when(slot < count)
        def _(slot=slot):
            store(0, slot).wait()

    if second:
        tell.wait()


def pack(second, destination, place, ranks, left, right, rows, cols):
    depth = TILE + 2 * RANK + (NOTE_ROWS if second else 0)
    tiles = pltpu.VMEM((DEPTH, TILE, 2 * RANK), BF16)
    return pl.pallas_call(
        functools.partial(pack_kernel, second),
        in_specs=[SCALAR] * 3 + [IN_HBM] * 2 + [HELD] * 2,
        out_specs=IN_HBM,
        out_shape=jax.ShapeDtypeStruct((GROUP, depth, TILE), BF16),
        scratch_shapes=[
            pltpu.SMEM((2, GROUP), jnp.int32),
            pltpu.SMEM((SENT,), jnp.int32),
            tiles,
            tiles,
            pltpu.VMEM((DEPTH, TILE + 2 * RANK, TILE), BF16),
            pltpu.VMEM((GROUP, NOTE_ROWS, TILE), BF16),
            pltpu.SemaphoreType.DMA((DEPTH, 2)),
            pltpu.SemaphoreType.DMA((DEPTH,)),
            pltpu.SemaphoreType.DMA,
        ],
        compiler_params=pltpu.CompilerParams(vmem_limit_bytes=ALL_VMEM_BYTES),
        cost_estimate=pl.CostEstimate(
            flops=4 * SENT * TILE**3, bytes_accessed=16 * 2**20, transcendentals=0
        ),
    )(destination, place, ranks, left, right, rows, cols)


def add_at(out, place, real, imag):
    a = place // TS
    rows = pl.ds(pl.multiple_of(a * TILE, TILE), TILE)
    cols = pl.ds(pl.multiple_of((place - a * TS) * TILE, TILE), TILE)
    out[0, rows, cols] += real
    out[1, rows, cols] += imag


def add_own(out, place, left, right):
    real_side = jnp.concatenate([right[:, :RANK], -right[:, RANK:]], 1)
    imag_side = jnp.concatenate([right[:, RANK:], right[:, :RANK]], 1)
    contract = (((1,), (1,)), ((), ()))
    add_at(
        out,
        place,
        lax.dot_general(left, real_side, contract, preferred_element_type=F32),
        lax.dot_general(left, imag_side, contract, preferred_element_type=F32),
    )


def add_slots(out, places, slots, scratch, prepare):
    order, arrived, sems = scratch

    def sort(slot, count):
        mine = places[slot] >= 0

        @pl.when(mine)
        def _():
            order[count] = slot

        return count + mine.astype(jnp.int32)

    count = lax.fori_loop(0, GROUP, sort, 0)

    def fetch(p, held):
        source = slots.at[order[p], pl.ds(0, TILE + 2 * RANK)]
        return pltpu.make_async_copy(source, arrived.at[held], sems.at[held])

    for p in range(DEPTH):

        @pl.when(p < count)
        def _(p=p):
            fetch(p, p).start()

    prepare()

    def work(p, carry):
        held = p & (DEPTH - 1)
        fetch(p, held).wait()
        left = arrived[held, :TILE, :]
        top = arrived[held, TILE : TILE + RANK, :]
        bottom = arrived[held, TILE + RANK :, :]
        add_at(
            out,
            places[order[p]],
            dot(left, jnp.concatenate([top, -bottom], 0)),
            dot(left, jnp.concatenate([bottom, top], 0)),
        )

        @pl.when(p + DEPTH < count)
        def _():
            fetch(p + DEPTH, held).start()

        return carry

    lax.fori_loop(0, count, work, 0)


def add_scratch():
    return [
        pltpu.SMEM((GROUP,), jnp.int32),
        pltpu.VMEM((DEPTH, TILE + 2 * RANK, TILE), BF16),
        pltpu.SemaphoreType.DMA((DEPTH,)),
    ]


def first_kernel(places, own_places, before, own_left, own_right, slots, out, *scratch):
    def prepare():
        pltpu.sync_copy(before, out)

        def own_step(j, carry):
            add_own(out, own_places[j], own_left[j], own_right[j])
            return carry

        lax.fori_loop(0, own_left.shape[0], own_step, 0)

    add_slots(out, places, slots, scratch, prepare)


def tile_at(i, j):
    return slice(i * TILE, (i + 1) * TILE), slice(j * TILE, (j + 1) * TILE)


def get(ref, rows, cols):
    return ref[0, rows, cols], ref[1, rows, cols]


def put(ref, rows, cols, value):
    ref[0, rows, cols] = value[0]
    ref[1, rows, cols] = value[1]


def second_kernel(places, role, before, slots, inverse, out, *refs):
    along_row, along_col = refs[:HALVES], refs[HALVES : 2 * HALVES]

    sem, *scratch = refs[2 * HALVES :]
    fetch = pltpu.make_async_copy(before, out, sem)
    fetch.start()
    add_slots(out, places, slots, scratch, fetch.wait)

    @pl.when((role[0] == 0) & (role[1] == 0))
    def _():
        pivots = [cuts((inverse[p, 0], inverse[p, 1])) for p in range(TS)]
        for p in range(TS - 1):
            uppers = {j: cuts(get(out, *tile_at(p, j))) for j in range(p + 1, TS)}
            for i in range(p + 1, TS):
                factor = complex_dot(cuts(get(out, *tile_at(i, p))), pivots[p])
                put(out, *tile_at(i, p), factor)
                factor = cuts(factor)
                for j in range(p + 1, TS):
                    at = tile_at(i, j)
                    put(out, *at, minus(get(out, *at), complex_dot(factor, uppers[j])))
        lower = [get(out, *tile_at(i, j)) for i, j in ((1, 0), (2, 0), (2, 1))]
        lower = jnp.concatenate([jnp.concatenate(x, 1) for x in lower], 0)
        upper = [
            complex_dot(cuts(get(out, *tile_at(i, j))), pivots[j])
            for i, j in ((0, 1), (0, 2), (1, 2))
        ]
        upper = [jnp.concatenate([x[half] for x in upper], 1) for half in (0, 1)]
        for half in range(HALVES):
            store_piece(along_row[half], lower[half * LONG : (half + 1) * LONG])
            store_piece(along_col[half], upper[half])

    @pl.when((role[0] > 0) & (role[1] == 0))
    def _():
        for p in range(TS):
            pivot = cuts((inverse[p, 0], inverse[p, 1]))
            for i in range(TS):
                at = tile_at(i, p)
                put(out, *at, complex_dot(cuts(get(out, *at)), pivot))
        for half in range(HALVES):
            rows = slice(half * LONG, (half + 1) * LONG)
            store_piece(along_row[half], jnp.concatenate(get(out, rows, slice(0, TILE)), 1))

    @pl.when((role[0] == 0) & (role[1] > 0))
    def _():
        for half in range(HALVES):
            store_piece(along_col[half], out[half, :TILE, :])


ADD_COST = pl.CostEstimate(
    flops=4 * GROUP * TILE**3, bytes_accessed=20 * 2**20, transcendentals=0
)


def add_first(places, own_places, before, own_left, own_right, slots):
    return pl.pallas_call(
        first_kernel,
        in_specs=[SCALAR, SCALAR, IN_HBM, HELD, HELD, IN_HBM],
        out_specs=HELD,
        out_shape=jax.ShapeDtypeStruct(before.shape, F32),
        scratch_shapes=add_scratch(),
        compiler_params=pltpu.CompilerParams(vmem_limit_bytes=MORE_VMEM_BYTES),
        cost_estimate=ADD_COST,
    )(places, own_places, before, own_left, own_right, slots)


def row_shape(panels):
    return (SIDE // HALVES + CODE_ROWS, 2 * TILE * panels)


def col_shape(panels):
    return (2 * TILE * panels // HALVES + CODE_ROWS, SIDE)


def coded(shape):
    return jax.ShapeDtypeStruct(shape, jnp.int16)


def pieces_of(panels):
    return [coded(row_shape(panels))] * HALVES + [coded(col_shape(panels))] * HALVES


def add_second(places, role, before, slots, inverse):
    return pl.pallas_call(
        second_kernel,
        in_specs=[SCALAR, SCALAR, IN_HBM, IN_HBM, HELD],
        out_specs=[HELD] * (1 + 2 * HALVES),
        out_shape=[jax.ShapeDtypeStruct(before.shape, F32)] + pieces_of(1),
        scratch_shapes=[pltpu.SemaphoreType.DMA] + add_scratch(),
        compiler_params=pltpu.CompilerParams(vmem_limit_bytes=MORE_VMEM_BYTES),
        cost_estimate=ADD_COST,
    )(places, role, before, slots, inverse)


def scales(code_rows):
    return jnp.exp(code_rows[:1].astype(jnp.int32).astype(F32) * LOG_STEP)


def unpack(refs, place, high, low):
    one, three, plus, minus = refs
    half = one.shape[0] - CODE_ROWS
    for at, pair in ((1, (one, plus)), (2, (plus, minus)), (3, (minus, three))):

        @pl.when(place == at)
        def _(pair=pair):
            for which, ref in enumerate(pair):
                scale = scales(ref[half:, :])

                def chunk(i, carry, ref=ref, scale=scale, which=which):
                    rows = pl.ds(pl.multiple_of(i * CHUNK, CHUNK), CHUNK)
                    into = pl.ds(pl.multiple_of(which * half + i * CHUNK, CHUNK), CHUNK)
                    values = ref[rows, :].astype(jnp.int32).astype(F32) * scale
                    high[into, :], low[into, :] = cut(values)
                    return carry

                lax.fori_loop(0, half // CHUNK, chunk, 0)


def trailing(block, out, rows, left, right):
    panels = left[0].shape[1] // (2 * TILE)

    def turned(x, imag):
        parts = []
        for p in range(panels):
            a = x[rows, 2 * p * TILE : (2 * p + 1) * TILE]
            b = x[rows, (2 * p + 1) * TILE : (2 * p + 2) * TILE]
            parts += [b, a] if imag else [a, -b]
        return jnp.concatenate(parts, 1)

    for half in (0, 1):
        a = [turned(x, half == 1) for x in left]
        for j in range(TS):
            cols = slice(j * TILE, (j + 1) * TILE)
            product = dot_cut(a, [x[:, cols] for x in right])
            out[half, rows, cols] = block[half, rows, cols] - product


def piece_scratch(panels):
    return [pltpu.VMEM((SIDE, 2 * TILE * panels), BF16)] * 2 + [
        pltpu.VMEM((2 * TILE * panels, SIDE), BF16)
    ] * 2


def panel_kernel(role, block, *refs):
    from_row, from_col = refs[:ARRIVALS], refs[ARRIVALS : 2 * ARRIVALS]
    out, *halves = refs[2 * ARRIVALS : 2 * ARRIVALS + 1 + HALVES]
    row_high, row_low, col_high, col_low = refs[2 * ARRIVALS + 1 + HALVES :]
    parts = [slice(t * TILE, (t + 1) * TILE) for t in range(TS)]

    @pl.when(role[1] > 0)
    def _():
        unpack(from_row, role[1], row_high, row_low)

    @pl.when(role[0] > 0)
    def _():
        unpack(from_col, role[0], col_high, col_low)

    @pl.when((role[0] == 0) & (role[1] == 0))
    def _():
        out[...] = block[...]

    @pl.when((role[0] > 0) & (role[1] == 0))
    def _():
        def tile(t):
            return [(col_high[rows, parts[t]], col_low[rows, parts[t]]) for rows in parts[:2]]

        def chunk(i, carry):
            rows = pl.ds(pl.multiple_of(i * TILE, TILE), TILE)
            f0 = get(block, rows, parts[0])
            put(out, rows, parts[0], f0)
            f0 = cuts(f0)
            f1 = minus(get(block, rows, parts[1]), complex_dot(f0, tile(0)))
            put(out, rows, parts[1], f1)
            f2 = minus(get(block, rows, parts[2]), complex_dot(f0, tile(1)))
            put(out, rows, parts[2], minus(f2, complex_dot(cuts(f1), tile(2))))
            return carry

        lax.fori_loop(0, TS, chunk, 0)
        for which, ref in enumerate(halves):
            half = which ^ (role[0] == ROW_TURNED).astype(jnp.int32)
            rows = pl.ds(pl.multiple_of(half * LONG, LONG), LONG)
            wide = [x for cols in parts[1:] for x in get(out, rows, cols)]
            store_piece(ref, jnp.concatenate(wide, 1))

    @pl.when((role[0] == 0) & (role[1] > 0))
    def _():
        def tile(t):
            return [(row_high[parts[t], cols], row_low[parts[t], cols]) for cols in parts[:2]]

        def chunk(j, carry):
            cols = pl.ds(pl.multiple_of(j * TILE, TILE), TILE)
            p0 = get(block, parts[0], cols)
            put(out, parts[0], cols, p0)
            p0 = cuts(p0)
            p1 = minus(get(block, parts[1], cols), complex_dot(tile(0), p0))
            put(out, parts[1], cols, p1)
            p2 = minus(get(block, parts[2], cols), complex_dot(tile(1), p0))
            put(out, parts[2], cols, minus(p2, complex_dot(tile(2), cuts(p1))))
            return carry

        lax.fori_loop(0, TS, chunk, 0)
        for which, ref in enumerate(halves):
            half = which ^ (role[1] == COL_TURNED).astype(jnp.int32)
            rows = pl.ds(pl.multiple_of((half + 1) * TILE, TILE), TILE)
            tall = jnp.concatenate(get(out, rows, slice(0, SIDE)), 0)
            rest = jnp.concatenate([tall[LONG:, cols] for cols in parts], 0)
            store_piece(ref, jnp.concatenate([tall[:LONG], rest], 1))

    @pl.when((role[0] > 0) & (role[1] > 0))
    def _():
        def chunk(i, carry):
            rows = pl.ds(pl.multiple_of(i * TILE, TILE), TILE)
            trailing(block, out, rows, (row_high, row_low), (col_high, col_low))
            return carry

        lax.fori_loop(0, TS, chunk, 0)


def panel(role, block, from_row, from_col):
    return pl.pallas_call(
        panel_kernel,
        in_specs=[SCALAR] + [HELD] * (1 + 2 * ARRIVALS),
        out_specs=[HELD] * (1 + HALVES),
        out_shape=[jax.ShapeDtypeStruct(block.shape, F32)] + [coded(row_shape(2))] * HALVES,
        scratch_shapes=piece_scratch(1),
        compiler_params=pltpu.CompilerParams(vmem_limit_bytes=VMEM_BYTES),
    )(role, block, *from_row, *from_col)


def trail_kernel(role, source, block, *refs):
    moved = refs[:MOVES]
    out, held, got, row_high, row_low, col_high, col_low, sem, sems, got_sems = refs[MOVES:]
    inner = (role[0] > 0) & (role[1] > 0)

    @pl.when(jnp.logical_not(inner))
    def _():
        store = pltpu.make_async_copy(block, out, sem)
        store.start()
        store.wait()

    @pl.when(inner)
    def _():
        first = (role[0] * 4 + role[1]) * 2 * HALVES
        for k in range(2 * HALVES):
            for m in range(MOVES):

                @pl.when(source[first + k] == m)
                def _(k=k, m=m):
                    pltpu.make_async_copy(moved[m], got.at[k], got_sems.at[k]).start()

        for k in range(2 * HALVES):
            pltpu.make_async_copy(moved[0], got.at[k], got_sems.at[k]).wait()
            scale = scales(got[k, LONG:, :])
            half = k % HALVES

            def chunk(i, carry, k=k, half=half, scale=scale):
                rows = pl.ds(pl.multiple_of(i * CHUNK, CHUNK), CHUNK)
                high, low = cut(got[k, rows, :].astype(jnp.int32).astype(F32) * scale)
                if k < HALVES:
                    into = pl.ds(pl.multiple_of(half * LONG + i * CHUNK, CHUNK), CHUNK)
                    row_high[into, :], row_low[into, :] = high, low
                else:
                    start = half * 2 * TILE + i * CHUNK
                    into = pl.ds(pl.multiple_of(start, CHUNK), CHUNK)
                    col_high[into, :], col_low[into, :] = high[:, :SIDE], low[:, :SIDE]
                    start = half * 2 * TILE + LONG + (i & 1) * CHUNK
                    into = pl.ds(pl.multiple_of(start, CHUNK), CHUNK)
                    cols = pl.ds(pl.multiple_of((i >> 1) * TILE, TILE), TILE)
                    col_high[into, cols], col_low[into, cols] = high[:, SIDE:], low[:, SIDE:]
                return carry

            lax.fori_loop(0, LONG // CHUNK, chunk, 0)

        def store(i):
            rows = pl.ds(pl.multiple_of(i * TILE, TILE), TILE)
            return pltpu.make_async_copy(held.at[:, rows, :], out.at[:, rows, :], sems.at[i])

        def chunk(i, carry):
            rows = pl.ds(pl.multiple_of(i * TILE, TILE), TILE)
            trailing(block, held, rows, (row_high, row_low), (col_high, col_low))
            store(i).start()
            return carry

        lax.fori_loop(0, TS, chunk, 0)
        for i in range(TS):
            store(i).wait()


def trail(role, source, block, moved):
    return pl.pallas_call(
        trail_kernel,
        in_specs=[SCALAR] * 2 + [HELD] * (1 + MOVES),
        out_specs=IN_HBM,
        out_shape=jax.ShapeDtypeStruct(block.shape, F32),
        scratch_shapes=[
            pltpu.VMEM(block.shape, F32),
            pltpu.VMEM((2 * HALVES,) + row_shape(2), jnp.int16),
        ]
        + piece_scratch(2)
        + [
            pltpu.SemaphoreType.DMA,
            pltpu.SemaphoreType.DMA((TS,)),
            pltpu.SemaphoreType.DMA((2 * HALVES,)),
        ],
        compiler_params=pltpu.CompilerParams(vmem_limit_bytes=VMEM_BYTES),
    )(role, source, block, *moved)


ROW_WAY = {1: 1, 2: 1, 3: 3}
COL_WAY = {1: 3, 2: 1, 3: 1}
ROW_TURNED, COL_TURNED = 3, 1
MOVES = 8


def ways(turn):
    def way(table, line):
        return 4 - table[line] if turn else table[line]

    return [(r, way(ROW_WAY, r)) for r in ROW_WAY], [(way(COL_WAY, c), c) for c in COL_WAY]


def move_all(halves):
    def move(array, pairs):
        pairs = [(4 * a + b, 4 * c + d) for (a, b), (c, d) in pairs]
        return lax.ppermute(array, ("row", "col"), pairs)

    out, on, late = [], [], []
    for turn in (0, 1):
        rows, cols = ways(turn)
        out.append([((r, 0), (r, c)) for r, c in rows] + [((0, c), (r, c)) for r, c in cols])
        on.append(
            [((r, c), (r, 2)) for r, c in rows] + [((r, c), (2, c)) for r, c in cols if c != 2]
        )
        late.append([((r, c), (2, c)) for r, c in cols if c == 2])
    first = [move(halves[turn], out[turn]) for turn in (0, 1)]
    second = [move(halves[1 - turn], out[turn]) for turn in (0, 1)]
    onward = [move(first[turn], on[turn]) for turn in (0, 1)]
    return first + second + onward + [move(first[turn], late[turn]) for turn in (0, 1)]


def sources():
    table = [0] * (16 * 2 * HALVES)

    def enter(row, col, slot, half, array):
        table[(row * 4 + col) * 2 * HALVES + slot * HALVES + half] = array

    for turn in (0, 1):
        rows, cols = ways(turn)
        for slot, devices in ((0, rows), (1, cols)):
            for r, c in devices:
                half = 0 if (c if slot == 0 else r) == 1 else 1
                enter(r, c, slot, half, turn)
                enter(r, c, slot, 1 - half, 2 + turn)
                middle = (r, 2) if slot == 0 else (2, c)
                both = slot == 1 and c == 2
                enter(*middle, slot, half, (6 if both else 4) + turn)
    return table


def broadcast(halves, axis):
    first = lax.axis_index(axis) == 0
    one = lax.ppermute(halves[0], axis, [(0, 1)])
    three = lax.ppermute(halves[1], axis, [(0, 3)])
    plus = lax.ppermute(jnp.where(first, halves[1], one), axis, [(0, 1), (1, 2)])
    minus = lax.ppermute(jnp.where(first, halves[0], three), axis, [(0, 3), (3, 2)])
    return one, three, plus, minus


def body(
    parent_front,
    child_left,
    child_right,
    tile_ranks,
    destination,
    tile_place,
    row_source,
    col_source,
    own_left,
    own_right,
    own_place,
    pivot_inverse,
):
    joined = ("front", "row")
    role = jnp.stack([lax.axis_index("row"), lax.axis_index("col")]).astype(jnp.int32)

    def sent(second):
        slots = pack(
            second,
            destination,
            tile_place,
            tile_ranks,
            child_left,
            child_right,
            row_source,
            col_source,
        )
        return lax.all_to_all(slots, joined, split_axis=0, concat_axis=0, tiled=True)

    second_slots = sent(1)
    first_slots = sent(0)
    places = second_slots[:, TILE + 2 * RANK : TILE + 2 * RANK + 2, 0].astype(jnp.int32)

    block = add_first(places[:, 0], own_place, parent_front[0], own_left, own_right, second_slots)
    block, *pieces = add_second(places[:, 1], role, block, first_slots, pivot_inverse[0])
    from_row, from_col = broadcast(pieces[:HALVES], "col"), broadcast(pieces[HALVES:], "row")
    block, *halves = panel(role, block, from_row, from_col)
    return trail(role, jnp.array(sources(), jnp.int32), block, move_all(halves))[None]


def solution(mesh):
    joined = ("front", "row", "col")
    tiles = P(joined, None, None)
    return jax.shard_map(
        body,
        mesh=mesh,
        in_specs=(
            P("front", None, "row", "col"),
            tiles,
            tiles,
            P(joined),
            P(joined),
            P(joined),
            P(joined, None),
            P(joined, None),
            tiles,
            tiles,
            P(joined),
            P("front", None, None, None, None),
        ),
        out_specs=P("front", None, "row", "col"),
        check_vma=False,
    )
```
